256 devices in a mesh: dp: 32 (over x, y, core), ctx: 8 (over z).
Axes of the slice: x: 4, y: 4, z: 8, core: 2. Of those that a mesh axis runs over, the one named last changes fastest.
Arguments:
- queries: bfloat16 [32768, 32, 128], P(('ctx', 'dp')), may hold values from -8 to 8
- keys: bfloat16 [32768, 8, 128], P(('ctx', 'dp')), may hold values from -8 to 8
- values: bfloat16 [32768, 8, 128], P(('ctx', 'dp')), may hold values from -6 to 6
- doc_blocks: int32 [32], replicated, may hold values from 1 to 16, 256 in all
Outputs:
- attended: bfloat16 [32768, 32, 128], P(('ctx', 'dp'))
The draws below stay inside these ranges and needn't reach their ends.
Inputs may be any that keep to these rules, and one draw needn't show every extreme that they name: `doc_blocks`: lengths in blocks of 128 tokens; they sum to 256 and the longest is exactly 16.
All inputs are finite; a program needn't handle non-finite values.
Results may differ from the reference program's by a relative error of at most 0.0037.
Values may be sent and summed in bfloat16 or wider, within the bound.
A program may use at most 128 MiB of HBM per device.

```python
import math
import jax
import jax.numpy as jnp
import numpy as np
from jax import lax

QH = 32
KVH = 8
HD = 128
BLK = 128
TOK_DEV = 128
TOKENS = 32768
NBLK = 256
MAXDOC_BLK = 16
NDOCS = 32
N_DP = 32
N_CTX = 8


def draw_queries(key, part):
    key = jax.random.fold_in(key, 1)
    entries = jnp.clip(jax.random.normal(key, (TOKENS, QH, HD), jnp.float32), -6.0, 6.0)
    return entries.astype(jnp.bfloat16)


def draw_keys(key, part):
    key = jax.random.fold_in(key, 2)
    entries = jnp.clip(jax.random.normal(key, (TOKENS, KVH, HD), jnp.float32), -6.0, 6.0)
    return entries.astype(jnp.bfloat16)


def shard_levels(own_key, dims, split, smallest, top_value):
    factor_of, own = 1.0, jax.random.fold_in(own_key, 6)
    for dim, parts in split:
        heights = jnp.exp(jax.random.uniform(jax.random.fold_in(own, dim), (parts,), jnp.float32, smallest / len(split), top_value / len(split)))
        factor_of = factor_of * jnp.repeat(heights, dims[dim] // parts).reshape([-1 if axis == dim else 1 for axis in range(len(dims))])
    return factor_of


def length_profile(count, total, most, skew):
    portions = [(1 << 20) // math.isqrt(standing ** skew) + 1 for standing in range(2, count + 1)]
    spare, holding = total - most - (count - 1), [1] * (count - 1)
    while spare > 0:
        candidates = [i for i in range(count - 1) if holding[i] < most]
        pool, left = sum([portions[i] for i in candidates]), spare
        for i in candidates:
            more = min(most - holding[i], max(1, left * portions[i] // pool), spare)
            holding[i] = holding[i] + more
            spare = spare - more
    return np.array([most] + holding)


def ragged_sizes(key, number_of, total, limit, slope):
    if number_of == 2:
        one = jax.random.randint(key, (), max(1, total - limit), min(limit, total - 1) + 1)
        return jnp.stack([one, total - one])
    tallies = jnp.asarray(length_profile(number_of, total, limit, slope), jnp.int32)
    pairs = (number_of - 1) // 2
    source_of, taker = tallies[1:1 + 2 * pairs:2], tallies[2:2 + 2 * pairs:2]
    slack = jnp.minimum(source_of - 1, limit - taker)
    moved = jax.random.randint(jax.random.fold_in(key, 1), (pairs,), 0, 1 << 20) % (slack + 1)
    tallies = tallies.at[1:1 + 2 * pairs:2].set(source_of - moved).at[2:2 + 2 * pairs:2].set(taker + moved)
    return tallies[jax.random.permutation(jax.random.fold_in(key, 2), number_of)]


def bell_draw(stream_key, shape, scale, limit, pieces=(), kind=jnp.bfloat16):
    factor_of = shard_levels(stream_key, shape, pieces, -0.22, 0.18) if pieces else 1.0
    result = jax.random.normal(stream_key, shape, jnp.float32) * scale * factor_of
    return jnp.minimum(jnp.maximum(result, -limit), limit).astype(kind)


def setup_inputs(seed: int = 0) -> dict:
    key_of = jax.random.split(jax.random.key(seed), 5)
    queries = draw_queries(jax.random.fold_in(key_of[4], 71), 0)
    keys = draw_keys(jax.random.fold_in(key_of[4], 71), 0)
    values = bell_draw(key_of[2], (TOKENS, KVH, HD), 1.0, 6.0, ((0, 256),))
    doc_blocks = ragged_sizes(key_of[3], NDOCS, NBLK, MAXDOC_BLK, 2).astype(jnp.int32)
    return dict(queries=queries, keys=keys, values=values, doc_blocks=doc_blocks)


def token_docs(doc_blocks, first_block, count, block):
    doc_ends = jnp.cumsum(doc_blocks, dtype=jnp.int32)
    blocks = first_block + jnp.arange(count, dtype=jnp.int32)
    owners = jnp.sum((doc_ends[None, :] <= blocks[:, None]).astype(jnp.int32), axis=1, dtype=jnp.int32)
    owners = jnp.where(blocks < 0, -1, owners)
    return jnp.repeat(owners, block)


def reference(queries, keys, values, doc_blocks):
    key_span = MAXDOC_BLK * BLK
    tile_rows = TOK_DEV * N_DP // N_CTX
    width = key_span + tile_rows
    group_size = QH // KVH
    key_docs = token_docs(doc_blocks, -MAXDOC_BLK, MAXDOC_BLK + NBLK, BLK)
    zero_rows = jnp.zeros((key_span, KVH, HD), jnp.bfloat16)
    key_buffer = jnp.concatenate([zero_rows, keys], axis=0)
    value_buffer = jnp.concatenate([zero_rows, values], axis=0)
    causal = jnp.arange(width)[None, :] <= key_span + jnp.arange(tile_rows)[:, None]
    score_scale = HD ** -0.5

    def one_tile(tile_index):
        offset = tile_index * tile_rows
        key_window = lax.dynamic_slice_in_dim(key_buffer, offset, width, 0)
        value_window = lax.dynamic_slice_in_dim(value_buffer, offset, width, 0)
        window_docs = lax.dynamic_slice_in_dim(key_docs, offset, width, 0)
        query_docs = lax.dynamic_slice_in_dim(key_docs, offset + key_span, tile_rows, 0)
        query_tile = lax.dynamic_slice_in_dim(queries, offset, tile_rows, 0)
        query_tile = query_tile.reshape(tile_rows, KVH, group_size, HD)
        allowed = (window_docs[None, :] == query_docs[:, None]) & causal
        scores = jnp.einsum("qgrd,kgd->grqk", query_tile.astype(jnp.float32), key_window.astype(jnp.float32)) * score_scale
        scores = jnp.where(allowed[None, None], scores, -jnp.inf)
        row_max = jnp.max(scores, axis=3, keepdims=True)
        weights = jnp.exp(scores - row_max)
        totals = jnp.sum(weights, axis=3)
        rounded = lax.optimization_barrier(weights.astype(jnp.bfloat16)).astype(jnp.float32)
        combined = jnp.einsum("grqk,kgd->qgrd", rounded, value_window.astype(jnp.float32))
        return (combined / jnp.transpose(totals, (2, 0, 1))[..., None]).astype(jnp.bfloat16)

    tiles = lax.map(one_tile, jnp.arange(TOKENS // tile_rows, dtype=jnp.int32))
    return tiles.reshape(TOKENS, QH, HD)
```

```python
import jax
import jax.numpy as jnp
from jax import lax
from jax.experimental import pallas as pl
from jax.experimental.pallas import tpu as pltpu
from jax.sharding import PartitionSpec as P

PIECES = 4
SEND_ORDER = (3, 0, 1, 2)
STEPS = (
    (215088, 5445680, 5445680, 202800),
    (2115584, 8389172, 8389428, 3359795),
    (6500401, 2114817, 2114817, 4200448),
    (2181136, 8454707, 8454707, 3162115),
    (2109697, 2180369, 2180369, 4266000),
    (149536, 8519683, 8519683, 3227667),
    (204817, 3294241, 2244897, 4331552),
    (229431, 8242, 4399635, 3294755),
    (6369569, 229429, 2326581, 28722),
    (6434824, 21523, 4202530, 3375159),
    (94517, 2241032, 2129925, 217349),
    (4202520, 1134626, 73763, 3178550),
    (159751, 73752, 98325, 1134594),
    (139304, 1200182, 151607, 3244055),
    (24837, 2322472, 2261046, 24594),
    (222226, 28695, 24583, 3309607),
    (90389, 2256902, 94230, 151586),
    (155685, 155670, 2256934, 155670),
)
OWN_SENDS = (
    (15, 13, 13, 12),
    (15, 13, 13, 12),
    (15, 13, 13, 12),
    (15, 13, 13, 12),
)
SENT = (
    (9, 10, 9, 8),
    (10, 9, 9, 8),
    (9, 10, 9, 8),
    (10, 9, 9, 8),
)
DIRS = 4
BLK = 128
HD = 128
LOG2E = 1.4426950408889634
MASKED = -1e30
MESH = pl.DeviceIdType.MESH


def of_y(y, row):
    value = jnp.int32(row[3])
    for i in range(3):
        value = jnp.where(y == i, jnp.int32(row[i]), value)
    return value


def kernel(
    q_ref, k_ref, v_ref, docs_ref, o_ref,
    own, sib, transit, qf, kf, vf, qs, acc, top,
    send_sem, pair_sem, own_sem, sib_sem, transit_sem,
):
    tokens, q_heads, _ = q_ref.shape
    kv_heads = k_ref.shape[1]
    group = q_heads // kv_heads
    rows = group * tokens
    per_part = kv_heads // PIECES
    parts = PIECES
    dp = lax.axis_index("dp")
    z = lax.axis_index("ctx")
    x, y, core = dp // 8, (dp // 2) % 4, dp % 2

    def at(to_x, to_y, to_z, to_core):
        return ((to_x % 4) * 8 + (to_y % 4) * 2 + to_core, to_z % 8)

    def one_if(condition):
        return jnp.where(condition, jnp.int32(1), jnp.int32(0))

    up = at(x, y + 1, z, core)
    down = at(x, y + 3, z, core)
    ahead = at(x + 1, y, z + one_if(x == 3), core)
    behind = at(x + 3, y, z + 8 - one_if(x == 0), core)
    through = at(x + 3, y, z, core)
    through_from = at(x + 1, y, z, core)
    beyond = at(x + 3, y, z + one_if((x == 1) | (x == 2)), core)
    beyond_from = at(x + 1, y, z + 8 - one_if(x <= 1), core)
    pair = at(x, y, z, 1 - core)
    targets = (up, down, ahead)
    shifts = (jnp.where(y == 3, jnp.int32(-3), jnp.int32(1)), jnp.where(y == 0, jnp.int32(3), jnp.int32(-1)), jnp.int32(4))

    kf[...] = k_ref[...].astype(jnp.float32).reshape(tokens * kv_heads, HD)
    vf[...] = v_ref[...].astype(jnp.float32).reshape(tokens * kv_heads, HD)
    for p in range(parts):
        for i in range(per_part):
            head = pl.ds(p * per_part + i, tokens, stride=kv_heads)
            own[p, pl.ds(i * BLK, BLK), :] = kf[head, :].astype(jnp.bfloat16)
            own[p, pl.ds((per_part + i) * BLK, BLK), :] = vf[head, :].astype(jnp.bfloat16)

    barrier = pltpu.get_barrier_semaphore()
    friends = (up, down, ahead, behind, through, through_from, beyond, beyond_from, pair)
    for friend in friends:
        pl.semaphore_signal(barrier, inc=1, device_id=friend, device_id_type=MESH)
    pl.semaphore_wait(barrier, len(friends))

    def send(src, dst, sem, landed, device):
        pltpu.make_async_remote_copy(
            src_ref=src, dst_ref=dst, send_sem=sem, recv_sem=landed, device_id=device, device_id_type=MESH
        ).start()

    def pass_on(k, p, bits):
        slot = k * parts + p
        for d in range(3):
            @pl.when((bits >> d) % 2 == 1)
            def _():
                to = (k + shifts[d]) * parts + p
                send(own.at[slot], own.at[to], send_sem.at[d], own_sem.at[to], targets[d])
        send(own.at[slot], sib.at[slot], pair_sem, sib_sem.at[slot], pair)

    def await_copy(ref, sem):
        pltpu.make_async_copy(ref, ref, sem).wait()

    for p in SEND_ORDER:
        bits = of_y(y, OWN_SENDS[p])
        send(own.at[p], transit.at[p], send_sem.at[3], transit_sem.at[p], through)
        pass_on(0, p, bits)

    scale = LOG2E * HD**-0.5
    qf[...] = q_ref[...].astype(jnp.float32).reshape(tokens * q_heads, HD)
    for g in range(kv_heads):
        for r in range(group):
            scaled = qf[pl.ds(g * group + r, tokens, stride=q_heads), :] * scale
            high = scaled.astype(jnp.bfloat16)
            qs[g, pl.ds(r * tokens, tokens), pl.ds(0, HD)] = high
            qs[g, pl.ds(r * tokens, tokens), pl.ds(HD, HD)] = (scaled - high.astype(jnp.float32)).astype(jnp.bfloat16)

    block = z * 32 + dp
    end = jnp.int32(0)
    start = jnp.int32(0)
    for i in range(docs_ref.shape[0]):
        end = end + docs_ref[i]
        start = jnp.where(end <= block, end, start)
    reach = block - start

    def bias_of(back):
        return jnp.where((back >= 0) & (back <= reach), jnp.float32(0), jnp.float32(MASKED))

    def sib_back(k):
        return 2 * k + 2 * core - 1

    ones = jnp.ones((2 * BLK, HD), jnp.bfloat16)

    def attend(k, p, bias, first):
        slot = k * parts + p
        for i in range(per_part):
            g = p * per_part + i
            at_keys, at_values = pl.ds(i * BLK, BLK), pl.ds((per_part + i) * BLK, BLK)
            keys = jnp.concatenate([own[slot, at_keys, :], sib[slot, at_keys, :]], axis=0)
            keys = jnp.concatenate([keys, keys], axis=1)
            values = jnp.concatenate([own[slot, at_values, :], sib[slot, at_values, :]], axis=0)
            values = jnp.concatenate([values, ones], axis=1)
            scores = lax.dot_general(
                qs[g], keys, (((1,), (1,)), ((), ())), preferred_element_type=jnp.float32
            )
            scores = scores + bias
            peak = jnp.max(scores, axis=1, keepdims=True)
            if first:
                new_top = jnp.broadcast_to(peak, (rows, BLK))
            else:
                new_top = jnp.maximum(top[g], peak)
            weights = jnp.exp2(scores - jnp.concatenate([new_top, new_top], axis=1))
            summed = jnp.dot(weights.astype(jnp.bfloat16), values, preferred_element_type=jnp.float32)
            if first:
                acc[g] = summed
            else:
                shrink = jnp.exp2(top[g] - new_top)
                acc[g] = acc[g] * jnp.concatenate([shrink, shrink], axis=1) + summed
            top[g] = new_top

    column = lax.broadcasted_iota(jnp.int32, (tokens, 2 * BLK), 1)
    row = lax.broadcasted_iota(jnp.int32, (tokens, 2 * BLK), 0)
    near = jnp.where(
        column < BLK, jnp.where(column <= row, jnp.float32(0), jnp.float32(MASKED)), bias_of(sib_back(0))
    )
    near = jnp.concatenate([near] * group, axis=0)
    for p in SEND_ORDER:
        await_copy(sib.at[p], sib_sem.at[p])
        attend(0, p, near, True)

    lane = lax.broadcasted_iota(jnp.int32, (1, 2 * BLK), 1)

    def attend_far(k, p):
        slot = k * parts + p
        await_copy(sib.at[slot], sib_sem.at[slot])
        bias = jnp.where(lane < BLK, bias_of(2 * k), bias_of(sib_back(k)))
        attend(k, p, bias, False)

    def step(word, half):
        code = (word >> (12 * half)) % 4096
        k, p, bits = code % 16, (code // 16) % 16, code // 256

        @pl.when(k == 0)
        def _():
            await_copy(transit.at[p], transit_sem.at[p])
            to = 8 * parts + p
            send(transit.at[p], own.at[to], send_sem.at[3], own_sem.at[to], beyond)

        @pl.when(k > 0)
        def _():
            slot = k * parts + p
            await_copy(own.at[slot], own_sem.at[slot])
            pass_on(k, p, bits)
        return k, p

    def word_at(index):
        value = jnp.int32(0)
        for i, entry in enumerate(STEPS):
            value = jnp.where(index == i, of_y(y, entry), value)
        return value

    def body(s, before):
        k, p = step(word_at(s // 2), s % 2)

        @pl.when(before[0] > 0)
        def _():
            attend_far(*before)
        return k, p

    last = lax.fori_loop(0, 9 * parts, body, (jnp.int32(0), jnp.int32(0)))

    @pl.when(last[0] > 0)
    def _():
        attend_far(*last)

    for g in range(kv_heads):
        for r in range(group):
            at_rows = pl.ds(r * tokens, tokens)
            result = acc[g, at_rows, pl.ds(0, HD)] / acc[g, at_rows, pl.ds(HD, HD)]
            qf[pl.ds(g * group + r, tokens, stride=q_heads), :] = result
    o_ref[...] = qf[...].reshape(tokens, q_heads, HD).astype(jnp.bfloat16)

    for i in range(4):
        @pl.when(y == i)
        def _():
            for d in range(DIRS):
                sent = own.at[pl.ds(0, SENT[i][d])]
                await_copy(sent, send_sem.at[d])
    await_copy(own, pair_sem)


def on_device(queries, keys, values, doc_blocks):
    tokens, q_heads, _ = queries.shape
    kv_heads = keys.shape[1]
    rows = q_heads // kv_heads * tokens
    part_rows = 2 * (kv_heads // PIECES) * BLK
    vmem = pl.BlockSpec(memory_space=pltpu.VMEM)
    return pl.pallas_call(
        kernel,
        out_shape=jax.ShapeDtypeStruct(queries.shape, jnp.bfloat16),
        in_specs=[vmem, vmem, vmem, pl.BlockSpec(memory_space=pltpu.SMEM)],
        out_specs=vmem,
        scratch_shapes=[
            pltpu.VMEM((9 * PIECES, part_rows, HD), jnp.bfloat16),
            pltpu.VMEM((9 * PIECES, part_rows, HD), jnp.bfloat16),
            pltpu.VMEM((PIECES, part_rows, HD), jnp.bfloat16),
            pltpu.VMEM((tokens * q_heads, HD), jnp.float32),
            pltpu.VMEM((tokens * kv_heads, HD), jnp.float32),
            pltpu.VMEM((tokens * kv_heads, HD), jnp.float32),
            pltpu.VMEM((kv_heads, rows, 2 * HD), jnp.bfloat16),
            pltpu.VMEM((kv_heads, rows, 2 * HD), jnp.float32),
            pltpu.VMEM((kv_heads, rows, BLK), jnp.float32),
            pltpu.SemaphoreType.DMA((DIRS,)),
            pltpu.SemaphoreType.DMA,
            pltpu.SemaphoreType.DMA((9 * PIECES,)),
            pltpu.SemaphoreType.DMA((9 * PIECES,)),
            pltpu.SemaphoreType.DMA((PIECES,)),
        ],
        compiler_params=pltpu.CompilerParams(
            collective_id=0, has_side_effects=True, vmem_limit_bytes=48 << 20
        ),
        name="attend",
    )(queries, keys, values, doc_blocks)


def solution(mesh):
    placed = P(("ctx", "dp"), None, None)
    return jax.shard_map(
        on_device,
        mesh=mesh,
        in_specs=(placed, placed, placed, P()),
        out_specs=placed,
        check_vma=False,
    )
```

```python
import jax
import jax.numpy as jnp
from jax import lax
from jax.experimental import pallas as pl
from jax.experimental.pallas import tpu as pltpu
from jax.sharding import PartitionSpec as P

STEPS = (
    (1114240, 2621984, 2097296, 6291600, 2162864, 4259968, 6358528, 6358528),
    (656384, 2294416, 6423568, 2163744, 2229248, 2228400, 6489632, 6422593),
    (2294016, 1459200, 2293888, 525360, 4260352, 2098224, 462931, 6488177),
    (721936, 1048752, 721056, 2294432, 332832, 332432, 299076, 278631),
    (5440800, 4326672, 278593, 720969, 299092, 409689, 540947, 540745),
    (2097225, 1704004, 1065049, 267280, 655764, 1196153, 344131, 274945),
    (364660, 345136, 398336, 430148, 1459248, 2293905, 1654873, 344145),
    (430736, 475440, 430180, 332036, 2293905, 4428825, 405764, 1654873),
    (266307, 364617, 4391204, 495700, 267273, 4194628, 430180, 2298151),
    (496160, 1065027, 1523825, 1454356, 397394, 1392705, 471204, 340228),
    (331875, 790633, 2162771, 463361, 364612, 398368, 475221, 430180),
    (2109569, 340089, 528739, 725348, 1388804, 463008, 1261689, 405924),
    (472073, 4231444, 4297265, 4231697, 2101380, 1409140, 1196181, 475218),
    (1261793, 331874, 4362401, 274804, 430193, 1540609, 737587, 737401),
    (4297233, 406553, 274505, 4362369, 524355, 671827, 4231729, 472073),
    (335940, 1261793, 495697, 364641, 496146, 299553, 4296801, 807961),
    (4362803, 4362771, 1393153, 4427921, 589939, 2297958, 336937, 1262633),
    (401492, 987251, 2232402, 606291, 475681, 1262601, 4428307, 479303),
    (2232579, 4428322, 479298, 1126947, 405832, 430194, 283139, 4428305),
    (410681, 295171, 4231512, 659525, 4297265, 4362307, 295029, 356449),
    (2170993, 360739, 426082, 270897, 528498, 270611, 557237, 2171080),
    (294983, 2367570, 4427847, 294997, 1258537, 528483, 487971, 413960),
    (2236707, 356659, 606504, 4296791, 282690, 282706, 1409089, 487896),
    (360533, 417896, 1077777, 487528, 1262649, 2302113, 332321, 348648),
    (426103, 807032, 741445, 401923, 352354, 413781, 1081704, 741880),
    (414003, 872519, 467045, 491784, 413857, 401585, 356422, 270406),
    (340088, 352326, 471112, 2232453, 2105521, 295029, 2171128, 401510),
    (352882, 422117, 286840, 1142898, 360565, 426099, 270648, 483414),
    (806999, 483573, 356437, 610407, 1147426, 483398, 417863, 114),
    (421990, 467063, 422006, 479528, 356456, 352327, 401511, 0),
    (286965, 0, 487510, 1273971, 491816, 421975, 544869, 0),
    (270454, 0, 102, 335960, 1142887, 119, 467062, 0),
    (0, 0, 0, 291128, 348472, 0, 86, 0),
    (0, 0, 0, 286821, 290886, 0, 0, 0),
    (0, 0, 0, 417878, 483623, 0, 0, 0),
    (0, 0, 0, 118, 487526, 0, 0, 0),
)
OPEN = (10, 5, 8, 8, 7, 7, 4, 2)
MOST = 12
PARTS = 4
BACK = 8
THROUGH = 9
DIRS = 4
BLK = 128
HD = 128
LOG2E = 1.4426950408889634
MASKED = -1e30
MESH = pl.DeviceIdType.MESH


def kernel(
    q_hbm, k_hbm, v_hbm, docs_hbm, o_ref,
    q_in, k_in, v_in, docs, parts, give_kv, give_q, give_out, qx, qf, kf, vf, qs, acc, top, even, odd,
    load_sem, send_sem, part_sem, kv_send, kv_sem, q_send, q_sem, out_send, out_sem,
):
    tokens, q_heads, _ = q_in.shape
    kv_heads = k_in.shape[1]
    group = q_heads // kv_heads
    rows = group * tokens
    dp = lax.axis_index("dp")
    z = lax.axis_index("ctx")
    planes = lax.axis_size("ctx")
    x, y, core = dp // 8, (dp // 2) % 4, dp % 2
    chip = dp // 2
    other = 1 - core

    def one_if(condition):
        return jnp.where(condition, jnp.int32(1), jnp.int32(0))

    def at(to_x, to_y, to_z, to_core):
        return ((to_x % 4) * 8 + (to_y % 4) * 2 + to_core, to_z)

    loads = [
        pltpu.make_async_copy(src, dst, load_sem.at[i])
        for i, (src, dst) in enumerate(((k_hbm, k_in), (v_hbm, v_in), (q_hbm, q_in), (docs_hbm, docs)))
    ]
    for load in loads:
        load.start()

    over_ahead = one_if(x == 3)
    over_beyond = one_if((x == 1) | (x == 2))
    has_ahead = z + over_ahead < planes
    has_behind = z - one_if(x == 0) >= 0
    has_beyond = z + over_beyond < planes
    has_beyond_from = z - one_if(x <= 1) >= 0
    has_through = z + one_if(x >= 2) < planes
    pair = at(x, y, z, other)
    up = at(x, y + 1, z, core)
    down = at(x, y + 3, z, core)
    ahead = at(x + 1, y, z + over_ahead, core)
    through = at(x + 3, y, z, core)

    barrier = pltpu.get_barrier_semaphore()

    def greet(device):
        pl.semaphore_signal(barrier, inc=1, device_id=device, device_id_type=MESH)

    for friend in (pair, up, down, through, at(x + 1, y, z, core)):
        greet(friend)
    maybe = (
        (has_ahead, ahead),
        (has_behind, at(x + 3, y, z - one_if(x == 0), core)),
        (has_beyond, at(x + 3, y, z + over_beyond, core)),
        (has_beyond_from, at(x + 1, y, z - one_if(x <= 1), core)),
    )
    greeted = jnp.int32(5)
    for there, friend in maybe:
        greeted = greeted + one_if(there)
        pl.when(there)(lambda friend=friend: greet(friend))

    loads[0].wait()
    kf[...] = k_in[...].astype(jnp.float32).reshape(tokens * kv_heads, HD)
    loads[1].wait()
    vf[...] = v_in[...].astype(jnp.float32).reshape(tokens * kv_heads, HD)
    mine = pl.multiple_of(core * 2 * BLK, 2 * BLK)
    for p in range(PARTS):
        head = pl.ds(other * PARTS + p, tokens, stride=kv_heads)
        give_kv[p, pl.ds(0, BLK), :] = kf[head, :].astype(jnp.bfloat16)
        give_kv[p, pl.ds(BLK, BLK), :] = vf[head, :].T.astype(jnp.bfloat16)
    for p in range(PARTS):
        head = pl.ds(core * PARTS + p, tokens, stride=kv_heads)
        parts[p, pl.ds(mine, BLK), :] = kf[head, :].astype(jnp.bfloat16)
        parts[p, pl.ds(mine + BLK, BLK), :] = vf[head, :].T.astype(jnp.bfloat16)

    pl.semaphore_wait(barrier, greeted)

    def send(src, dst, sem, landed, device):
        pltpu.make_async_remote_copy(
            src_ref=src, dst_ref=dst, send_sem=sem, recv_sem=landed, device_id=device, device_id_type=MESH
        ).start()

    def await_copy(ref, sem):
        pltpu.make_async_copy(ref, ref, sem).wait()

    for p in range(PARTS):
        send(give_kv.at[p], parts.at[p, pl.ds(mine, 2 * BLK)], kv_send, kv_sem.at[p], pair)

    loads[2].wait()
    qf[...] = q_in[...].astype(jnp.float32).reshape(tokens * q_heads, HD)

    def queries_of(p, r, side):
        return qf[pl.ds((side * PARTS + p) * group + r, tokens, stride=q_heads), :].T

    for p in range(PARTS):
        for r in range(group):
            give_q[p, :, pl.ds(r * tokens, tokens)] = queries_of(p, r, other).astype(jnp.bfloat16)
        send(give_q.at[p], qx.at[p], q_send, q_sem.at[p], pair)

    scale = LOG2E * HD**-0.5

    def put_queries(p, at_rows, value):
        scaled = value * scale
        high = scaled.astype(jnp.bfloat16)
        qs[p, pl.ds(0, HD), at_rows] = high
        qs[p, pl.ds(HD, HD), at_rows] = (scaled - high.astype(jnp.float32)).astype(jnp.bfloat16)

    for p in range(PARTS):
        for r in range(group):
            put_queries(p, pl.ds(pl.multiple_of(core * rows + r * tokens, tokens), tokens), queries_of(p, r, core))

    loads[3].wait()
    reach = []
    for b in range(2):
        block = (z * 16 + chip) * 2 + b
        end = jnp.int32(0)
        start = jnp.int32(0)
        for i in range(docs.shape[0]):
            end = end + docs[i]
            start = jnp.where(end <= block, end, start)
        reach.append(block - start)

    def bias_of(back, b):
        return jnp.where(back <= reach[b], jnp.float32(0), jnp.float32(MASKED))

    ones = jnp.ones((16, 2 * BLK), jnp.bfloat16)

    def score(slot, p, into):
        keys = jnp.concatenate([parts[slot, pl.ds(0, BLK), :], parts[slot, pl.ds(2 * BLK, BLK), :]], axis=0)
        keys = jnp.concatenate([keys, keys], axis=1)
        for b in range(2):
            at_rows = pl.ds(b * rows, rows)
            into[:, at_rows] = jnp.dot(keys, qs[p, :, at_rows], preferred_element_type=jnp.float32)

    def combine(slot, p, scores, biases, causal=None):
        values = jnp.concatenate([parts[slot, pl.ds(BLK, BLK), :], parts[slot, pl.ds(3 * BLK, BLK), :]], axis=1)
        values = jnp.concatenate([values, ones], axis=0)
        for b in range(2):
            at_rows = pl.ds(b * rows, rows)
            halves = [scores[pl.ds(h * BLK, BLK), at_rows] for h in range(2)]
            if causal is not None:
                halves[b] = halves[b] + causal
            peaks = [jnp.max(halves[h], axis=0, keepdims=True) + biases[b][h] for h in range(2)]
            new_top = jnp.maximum(peaks[0], peaks[1])
            if causal is None:
                old_top = top[p, pl.ds(0, 1), at_rows]
                new_top = jnp.maximum(old_top, new_top)
            weights = [jnp.exp2(halves[h] - (new_top - biases[b][h])).astype(jnp.bfloat16) for h in range(2)]
            summed = jnp.dot(values, jnp.concatenate(weights, axis=0), preferred_element_type=jnp.float32)
            if causal is None:
                acc[p, :, at_rows] = acc[p, :, at_rows] * jnp.exp2(old_top - new_top) + summed
            else:
                acc[p, :, at_rows] = summed
            top[p, pl.ds(0, 1), at_rows] = new_top

    def combine_back(k, p, scores):
        biases = [[bias_of(2 * k + b - h, b) for h in range(2)] for b in range(2)]
        combine(k * PARTS + p, p, scores, biases)

    shifts = (
        jnp.where(y == 3, jnp.int32(-3), jnp.int32(1)),
        jnp.where(y == 0, jnp.int32(3), jnp.int32(-1)),
        jnp.int32(4),
    )
    targets = (up, down, ahead)
    allowed = (True, True, has_ahead)

    def of_place(entry):
        value = jnp.int32(entry[7])
        for j in range(7):
            value = jnp.where(y * 2 + core == j, jnp.int32(entry[j]), value)
        return value

    def word_at(index):
        value = jnp.int32(0)
        for i, entry in enumerate(STEPS):
            value = jnp.where(index == i, of_place(entry), value)
        return value

    def step(s, counts):
        code = (word_at(s // 2) >> (12 * (s % 2))) % 4096
        k, p, waits, bits = code % 16, (code // 16) % 4, (code // 64) % 2, code // 128
        slot = k * PARTS + p
        here = (k == 0) | ((k == THROUGH) & has_beyond) | ((k != THROUGH) & ((z > 0) | (chip >= k)))

        @pl.when(here & (waits == 1))
        def _():
            await_copy(parts.at[slot], part_sem.at[slot])

        new_counts = []
        for d in range(3):
            go = here & ((bits >> d) % 2 == 1) & allowed[d]
            new_counts.append(counts[d] + one_if(go))

            @pl.when(go)
            def _():
                to = slot + shifts[d] * PARTS
                send(parts.at[slot], parts.at[to], send_sem.at[d], part_sem.at[to], targets[d])

        go = here & (bits // 8 == 1) & ((k == THROUGH) | has_through)
        new_counts.append(counts[3] + one_if(go))

        @pl.when(go)
        def _():
            to = jnp.where(k == THROUGH, BACK * PARTS + p, THROUGH * PARTS + p)
            device = at(x + 3, y, z + jnp.where(k == THROUGH, over_beyond, 0), core)
            send(parts.at[slot], parts.at[to], send_sem.at[3], part_sem.at[to], device)

        done, before_k, before_p = counts[4:]
        go = here & (waits == 1) & (k != THROUGH)

        @pl.when(go & (done == 0))
        def _():
            score(slot, p, even)

        @pl.when(go & (done % 2 == 1))
        def _():
            score(slot, p, odd)
            combine_back(before_k, before_p, even)

        @pl.when(go & (done > 0) & (done % 2 == 0))
        def _():
            score(slot, p, even)
            combine_back(before_k, before_p, odd)

        new_counts += [done + one_if(go), jnp.where(go, k, before_k), jnp.where(go, p, before_p)]
        return tuple(new_counts)

    for p in range(PARTS):
        await_copy(give_kv.at[p], kv_sem.at[p])

    def attend_own():
        key = lax.broadcasted_iota(jnp.int32, (BLK, rows), 0)
        query = lax.broadcasted_iota(jnp.int32, (BLK, rows), 1) % tokens
        causal = jnp.where(key <= query, jnp.float32(0), jnp.float32(MASKED))
        biases = [[jnp.float32(0), jnp.float32(MASKED)], [bias_of(1, 1), jnp.float32(0)]]
        for p in range(PARTS):
            await_copy(qx.at[p], q_sem.at[p])
            put_queries(p, pl.ds(pl.multiple_of(other * rows, rows), rows), qx[p].astype(jnp.float32))
        score(0, 0, even)
        for p in range(PARTS):
            if p + 1 < PARTS:
                score(p + 1, p + 1, (even, odd)[(p + 1) % 2])
            combine(p, p, (even, odd)[p % 2], biases, causal)

    zero = jnp.int32(0)
    opening = of_place(OPEN)
    state = lax.fori_loop(0, opening, step, (zero,) * 7)
    attend_own()
    state = lax.fori_loop(opening, 2 * len(STEPS), step, state)
    counts, (done, before_k, before_p) = state[:4], state[4:]
    for odd_last in range(2):
        @pl.when((done > 0) & (done % 2 == 1 - odd_last))
        def _():
            combine_back(before_k, before_p, (even, odd)[odd_last])

    def result(p, r, side):
        at_rows = pl.ds(pl.multiple_of(side * rows + r * tokens, tokens), tokens)
        return (acc[p, pl.ds(0, HD), at_rows] / acc[p, pl.ds(HD, 1), at_rows]).T.astype(jnp.bfloat16)

    for p in range(PARTS):
        for r in range(group):
            give_out[p, pl.ds(r * tokens, tokens), :] = result(p, r, other)
        send(give_out.at[p], o_ref.at[core * PARTS + p], out_send, out_sem, pair)
    for p in range(PARTS):
        for r in range(group):
            o_ref[core * PARTS + p, pl.ds(r * tokens, tokens), :] = result(p, r, core)

    for d in range(DIRS):
        for n in range(1, MOST + 1):
            @pl.when(counts[d] == n)
            def _():
                await_copy(parts.at[pl.ds(0, n)], send_sem.at[d])
    await_copy(give_kv, kv_send)
    await_copy(give_q, q_send)
    await_copy(give_out, out_send)
    await_copy(give_out, out_sem)


def on_device(queries, keys, values, doc_blocks):
    tokens, q_heads, _ = queries.shape
    kv_heads = keys.shape[1]
    group = q_heads // kv_heads
    rows = group * tokens
    bf16, f32 = jnp.bfloat16, jnp.float32
    anywhere = pl.BlockSpec(memory_space=pl.ANY)
    dma = pltpu.SemaphoreType.DMA
    by_head = pl.pallas_call(
        kernel,
        out_shape=jax.ShapeDtypeStruct((kv_heads, rows, HD), bf16),
        in_specs=[anywhere] * 4,
        out_specs=pl.BlockSpec(memory_space=pltpu.VMEM),
        scratch_shapes=[
            pltpu.VMEM(queries.shape, bf16),
            pltpu.VMEM(keys.shape, bf16),
            pltpu.VMEM(values.shape, bf16),
            pltpu.SMEM(doc_blocks.shape, jnp.int32),
            pltpu.VMEM(((THROUGH + 1) * PARTS, 4 * BLK, HD), bf16),
            pltpu.VMEM((PARTS, 2 * BLK, HD), bf16),
            pltpu.VMEM((PARTS, HD, rows), bf16),
            pltpu.VMEM((PARTS, rows, HD), bf16),
            pltpu.VMEM((PARTS, HD, rows), bf16),
            pltpu.VMEM((tokens * q_heads, HD), f32),
            pltpu.VMEM((tokens * kv_heads, HD), f32),
            pltpu.VMEM((tokens * kv_heads, HD), f32),
            pltpu.VMEM((PARTS, 2 * HD, 2 * rows), bf16),
            pltpu.VMEM((PARTS, HD + 16, 2 * rows), f32),
            pltpu.VMEM((PARTS, 8, 2 * rows), f32),
            pltpu.VMEM((2 * BLK, 2 * rows), f32),
            pltpu.VMEM((2 * BLK, 2 * rows), f32),
            dma((4,)),
            dma((DIRS,)),
            dma(((THROUGH + 1) * PARTS,)),
            dma,
            dma((PARTS,)),
            dma,
            dma((PARTS,)),
            dma,
            dma,
        ],
        compiler_params=pltpu.CompilerParams(
            collective_id=0, has_side_effects=True, vmem_limit_bytes=63 << 20
        ),
        name="attend",
    )(queries, keys, values, doc_blocks)
    by_head = by_head.reshape(q_heads, tokens, HD)
    return jnp.transpose(by_head, (1, 0, 2))


def solution(mesh):
    placed = P(("ctx", "dp"), None, None)
    return jax.shard_map(
        on_device,
        mesh=mesh,
        in_specs=(placed, placed, placed, P()),
        out_specs=placed,
        check_vma=False,
    )
```

```python
import jax
import jax.numpy as jnp
from jax import lax
from jax.experimental import pallas as pl
from jax.experimental.pallas import tpu as pltpu
from jax.sharding import PartitionSpec as P

STEPS = (
    (1073281, 1056899, 5243009, 1065091, 1073281, 1065089, 4194817, 4211201),
    (2113792, 6316288, 8398339, 4219392, 4219392, 4219392, 4211715, 8406019),
    (4211200, 8414720, 4210819, 12592128, 8397826, 8397824, 663621, 844288),
    (14705664, 1065729, 656384, 655488, 1049090, 9462274, 3285095, 565329),
    (1049601, 680961, 565351, 2228324, 656387, 581712, 2721831, 1189927),
    (819280, 6307940, 4235536, 4212772, 835653, 2228324, 655875, 4219212),
    (2229250, 8405139, 1091623, 827521, 17088784, 5302308, 3276871, 575590),
    (843906, 655463, 827463, 17080403, 1180161, 680037, 4235342, 2744786),
    (17072210, 2230308, 17080659, 2720531, 557157, 2252870, 1720675, 811525),
    (2105490, 1614412, 4251778, 582097, 2728275, 1099813, 4251727, 1704007),
    (4760140, 1712229, 671812, 713295, 17080837, 672072, 688398, 2228301),
    (2244709, 17096972, 2244708, 1237074, 843909, 843844, 1212499, 680454),
    (649255, 671814, 8405508, 565519, 581714, 4227346, 4325523, 1204299),
    (836292, 17080422, 647303, 557714, 590098, 8405120, 598290, 2383950),
    (2222117, 2236550, 2910244, 598115, 4325508, 565344, 557269, 696848),
    (574030, 557640, 1196559, 786706, 600103, 17096992, 2253321, 1220682),
    (680149, 17088786, 622945, 5316678, 663650, 2891920, 589911, 2203740),
    (2269702, 4825234, 1763430, 2383950, 622882, 4817028, 4259991, 4333666),
    (4786214, 647751, 4784462, 696415, 1106441, 745574, 4317276, 2326742),
    (2211932, 2203783, 696390, 1220705, 795140, 641062, 1777741, 1835527),
    (786631, 1081929, 598366, 2351620, 696390, 1269847, 770401, 4284693),
    (2703879, 786524, 704863, 802890, 778513, 688203, 614621, 1843470),
    (778313, 1122890, 688224, 1753610, 1065480, 2850901, 745568, 4276292),
    (688342, 720995, 729186, 2376206, 729375, 811141, 720966, 688216),
    (4268131, 794699, 720973, 5857497, 606732, 704607, 704602, 589917),
    (762134, 639069, 614491, 3883100, 4251801, 598114, 606303, 778334),
    (770264, 712802, 737373, 688221, 639265, 729165, 98, 729175),
    (802913, 688223, 606289, 770136, 1098250, 737368, 0, 745545),
    (614490, 745561, 92, 745544, 786709, 761937, 0, 90),
    (630875, 770133, 0, 77, 811534, 606287, 0, 0),
    (663639, 704602, 0, 0, 2211915, 94, 0, 0),
    (89, 0, 0, 0, 704596, 0, 0, 0),
    (0, 0, 0, 0, 745560, 0, 0, 0),
    (0, 0, 0, 0, 647260, 0, 0, 0),
    (0, 0, 0, 0, 737367, 0, 0, 0),
    (0, 0, 0, 0, 761950, 0, 0, 0),
)
UNITS = (
    (720, 659, 528, 528, 656, 592, 325, 465),
    (1106, 1040, 645, 979, 709, 647, 401, 517),
    (1356, 1228, 967, 1164, 1156, 1043, 652, 716),
    (1413, 1285, 1107, 1233, 1235, 1094, 784, 902),
    (1679, 1425, 1348, 1287, 1293, 1352, 839, 978),
    (1732, 1606, 1426, 1359, 1618, 1426, 974, 1039),
    (1998, 1682, 1807, 1431, 1671, 1476, 1123, 1187),
    (2054, 1992, 1955, 1490, 1800, 1888, 1170, 1223),
    (2133, 2052, 2145, 1669, 2057, 1925, 1231, 1296),
    (2195, 2317, 2188, 1796, 2146, 2209, 1428, 1357),
    (2440, 2375, 2327, 1891, 2193, 2316, 1491, 1555),
    (2524, 2447, 2382, 1929, 2316, 2459, 1801, 1611),
    (2631, 2633, 2440, 2080, 2593, 2574, 1877, 1742),
    (2720, 2780, 2502, 2118, 2630, 2647, 1924, 1941),
    (2826, 2848, 2581, 2254, 2709, 2763, 2135, 1994),
    (2889, 2890, 2654, 2399, 2847, 2836, 2184, 2140),
    (2975, 3043, 2697, 2453, 3097, 2901, 2396, 2274),
    (3030, 3096, 2783, 2529, 3210, 2972, 2509, 2390),
    (3092, 3147, 2838, 2762, 3470, 3107, 2585, 2592),
    (3171, 3233, 2912, 2850, 3744, 3167, 2657, 2849),
    (3357, 3293, 2964, 2966, 3875, 3222, 2718, 2884),
    (3416, 3342, 3042, 3161, 3915, 3298, 2781, 3032),
    (3486, 3426, 3097, 3211, 4052, 3337, 2827, 3092),
    (3553, 3479, 3149, 3292, 4118, 3405, 2912, 3165),
    (3618, 3551, 3224, 3354, 4184, 3481, 2971, 3208),
    (3674, 3604, 3291, 3421, 4251, 3544, 3014, 3294),
    (3723, 3673, 3339, 3476, 4316, 3610, 3096, 3359),
    (3803, 3739, 3421, 3544, 4367, 3665, 3162, 3415),
    (3853, 3797, 3482, 3614, 4439, 3741, 3222, 3481),
    (3927, 3870, 3537, 3656, 4506, 3791, 3295, 3529),
    (3985, 3930, 3594, 3739, 4574, 3850, 3338, 3611),
    (4057, 3990, 3676, 3789, 4637, 3934, 3426, 3674),
)
OPEN = (10, 9, 7, 7, 9, 8, 4, 5)
MOST = 13
PARTS = 4
BACK = 8
THROUGH = 9
DIRS = 5
BLK = 128
HD = 128
LOG2E = 1.4426950408889634
MASKED = -1e30
MESH = pl.DeviceIdType.MESH


def kernel(
    q_hbm, k_hbm, v_hbm, docs_hbm, o_ref,
    q_in, k_in, v_in, docs, parts, give_kv, give_q, give_out, qx, qf, kf, vf, qs, acc, top, even, odd,
    load_sem, send_sem, part_sem, kv_send, kv_sem, q_send, q_sem, out_send, out_sem,
):
    tokens, q_heads, _ = q_in.shape
    kv_heads = k_in.shape[1]
    group = q_heads // kv_heads
    rows = group * tokens
    dp = lax.axis_index("dp")
    z = lax.axis_index("ctx")
    planes = lax.axis_size("ctx")
    x, y, core = dp // 8, (dp // 2) % 4, dp % 2
    chip = dp // 2
    other = 1 - core

    def one_if(condition):
        return jnp.where(condition, jnp.int32(1), jnp.int32(0))

    def at(to_x, to_y, to_z, to_core):
        return ((to_x % 4) * 8 + (to_y % 4) * 2 + to_core, to_z)

    loads = [
        pltpu.make_async_copy(src, dst, load_sem.at[i])
        for i, (src, dst) in enumerate(((k_hbm, k_in), (v_hbm, v_in), (q_hbm, q_in), (docs_hbm, docs)))
    ]
    for load in loads:
        load.start()

    over_ahead = one_if(x == 3)
    over_beyond = one_if((x == 1) | (x == 2))
    has_ahead = z + over_ahead < planes
    has_behind = z - one_if(x == 0) >= 0
    has_beyond = z + over_beyond < planes
    has_beyond_from = z - one_if(x <= 1) >= 0
    has_through = z + one_if(x >= 2) < planes
    pair = at(x, y, z, other)
    up = at(x, y + 1, z, core)
    down = at(x, y + 3, z, core)
    ahead = at(x + 1, y, z + over_ahead, core)
    through = at(x + 3, y, z, core)

    last_here = PARTS * jnp.where(z > 0, jnp.int32(BACK), jnp.minimum(chip, BACK)) + PARTS - 1

    def clear(slot, c):
        parts[slot] = jnp.zeros((4 * BLK, HD), jnp.bfloat16)
        return c
    lax.fori_loop(last_here + 1, (BACK + 1) * PARTS, clear, 0)

    barrier = pltpu.get_barrier_semaphore()

    def greet(device):
        pl.semaphore_signal(barrier, inc=1, device_id=device, device_id_type=MESH)

    for friend in (pair, up, down, through, at(x + 1, y, z, core)):
        greet(friend)
    maybe = (
        (has_ahead, ahead),
        (has_behind, at(x + 3, y, z - one_if(x == 0), core)),
        (has_beyond, at(x + 3, y, z + over_beyond, core)),
        (has_beyond_from, at(x + 1, y, z - one_if(x <= 1), core)),
    )
    greeted = jnp.int32(5)
    for there, friend in maybe:
        greeted = greeted + one_if(there)
        pl.when(there)(lambda friend=friend: greet(friend))

    def of_place(entry):
        pairs = [jnp.where(core == 0, jnp.int32(entry[2 * i]), jnp.int32(entry[2 * i + 1])) for i in range(4)]
        return jnp.where(y < 2, jnp.where(y == 0, pairs[0], pairs[1]), jnp.where(y == 2, pairs[2], pairs[3]))

    steps = [of_place(entry) for entry in STEPS]
    units = [of_place(entry) for entry in UNITS]

    def pick(values, index):
        while len(values) > 1:
            low = (index & 1) == 0
            values = [
                jnp.where(low, values[i], values[i + 1]) if i + 1 < len(values) else values[i]
                for i in range(0, len(values), 2)
            ]
            index = index >> 1
        return values[0]

    loads[0].wait()
    kf[...] = k_in[...].astype(jnp.float32).reshape(tokens * kv_heads, HD)
    loads[1].wait()
    vf[...] = v_in[...].astype(jnp.float32).reshape(tokens * kv_heads, HD)
    mine = pl.multiple_of(core * 2 * BLK, 2 * BLK)
    for p in range(PARTS):
        head = pl.ds(other * PARTS + p, tokens, stride=kv_heads)
        give_kv[p, pl.ds(0, BLK), :] = kf[head, :].astype(jnp.bfloat16)
        give_kv[p, pl.ds(BLK, BLK), :] = vf[head, :].T.astype(jnp.bfloat16)
    for p in range(PARTS):
        head = pl.ds(core * PARTS + p, tokens, stride=kv_heads)
        parts[p, pl.ds(mine, BLK), :] = kf[head, :].astype(jnp.bfloat16)
        parts[p, pl.ds(mine + BLK, BLK), :] = vf[head, :].T.astype(jnp.bfloat16)

    pl.semaphore_wait(barrier, greeted)

    def send(src, dst, sem, landed, device):
        pltpu.make_async_remote_copy(
            src_ref=src, dst_ref=dst, send_sem=sem, recv_sem=landed, device_id=device, device_id_type=MESH
        ).start()

    def await_copy(ref, sem):
        pltpu.make_async_copy(ref, ref, sem).wait()

    for p in range(PARTS):
        send(give_kv.at[p], parts.at[p, pl.ds(mine, 2 * BLK)], kv_send, kv_sem.at[p], pair)

    loads[2].wait()
    qf[...] = q_in[...].astype(jnp.float32).reshape(tokens * q_heads, HD)

    def queries_of(p, r, side):
        return qf[pl.ds((side * PARTS + p) * group + r, tokens, stride=q_heads), :].T

    for p in range(PARTS):
        for r in range(group):
            give_q[p, :, pl.ds(r * tokens, tokens)] = queries_of(p, r, other).astype(jnp.bfloat16)
        send(give_q.at[p], qx.at[p], q_send, q_sem.at[p], pair)

    scale = LOG2E * HD**-0.5

    def put_queries(p, at_rows, value):
        scaled = value * scale
        high = scaled.astype(jnp.bfloat16)
        qs[p, pl.ds(0, HD), at_rows] = high
        qs[p, pl.ds(HD, HD), at_rows] = (scaled - high.astype(jnp.float32)).astype(jnp.bfloat16)

    for p in range(PARTS):
        for r in range(group):
            put_queries(p, pl.ds(pl.multiple_of(core * rows + r * tokens, tokens), tokens), queries_of(p, r, core))

    loads[3].wait()
    reach = []
    for b in range(2):
        block = (z * 16 + chip) * 2 + b
        end = jnp.int32(0)
        start = jnp.int32(0)
        for i in range(docs.shape[0]):
            end = end + docs[i]
            start = jnp.where(end <= block, end, start)
        reach.append(block - start)

    def bias_of(back, b):
        return jnp.where(back <= reach[b], jnp.float32(0), jnp.float32(MASKED))

    ones = jnp.ones((16, 2 * BLK), jnp.bfloat16)

    def score(slot, p, into):
        keys = jnp.concatenate([parts[slot, pl.ds(0, BLK), :], parts[slot, pl.ds(2 * BLK, BLK), :]], axis=0)
        keys = jnp.concatenate([keys, keys], axis=1)
        for b in range(2):
            at_rows = pl.ds(b * rows, rows)
            into[:, at_rows] = jnp.dot(keys, qs[p, :, at_rows], preferred_element_type=jnp.float32)

    def combine(slot, p, scores, biases, causal=None):
        values = jnp.concatenate([parts[slot, pl.ds(BLK, BLK), :], parts[slot, pl.ds(3 * BLK, BLK), :]], axis=1)
        values = jnp.concatenate([values, ones], axis=0)
        for b in range(2):
            at_rows = pl.ds(b * rows, rows)
            halves = [scores[pl.ds(h * BLK, BLK), at_rows] for h in range(2)]
            if causal is not None:
                halves[b] = halves[b] + causal
            peaks = [jnp.max(halves[h], axis=0, keepdims=True) + biases[b][h] for h in range(2)]
            new_top = jnp.maximum(peaks[0], peaks[1])
            if causal is None:
                old_top = top[p, pl.ds(0, 1), at_rows]
                new_top = jnp.maximum(old_top, new_top)
            weights = [jnp.exp2(halves[h] - (new_top - biases[b][h])).astype(jnp.bfloat16) for h in range(2)]
            summed = jnp.dot(values, jnp.concatenate(weights, axis=0), preferred_element_type=jnp.float32)
            if causal is None:
                acc[p, :, at_rows] = acc[p, :, at_rows] * jnp.exp2(old_top - new_top) + summed
            else:
                acc[p, :, at_rows] = summed
            top[p, pl.ds(0, 1), at_rows] = new_top

    def combine_back(code, scores):
        k, p = code >> 2, code & (PARTS - 1)
        biases = [[bias_of(2 * k + b - h, b) for h in range(2)] for b in range(2)]
        combine(code & 63, p, scores, biases)

    shifts = (
        PARTS * jnp.where(y == 3, jnp.int32(-3), jnp.int32(1)),
        PARTS * jnp.where(y == 0, jnp.int32(3), jnp.int32(-1)),
        4 * PARTS,
        THROUGH * PARTS,
        (BACK - THROUGH) * PARTS,
    )
    targets = (up, down, ahead, through, at(x + 3, y, z + over_beyond, core))
    open_ways = 3 + 4 * one_if(has_ahead) + 8 * one_if(has_through) + 16 * one_if(has_beyond)

    def step(s, sent):
        word = pick(steps, s >> 1) >> (13 * (s & 1))
        slot = word & 63
        here = (slot <= last_here) | ((slot >= THROUGH * PARTS) & has_beyond)
        ways = jnp.where(here, (word >> 7) & open_ways, 0)

        @pl.when(here & ((word & 64) != 0))
        def _():
            await_copy(parts.at[slot], part_sem.at[slot])

        @pl.when(ways != 0)
        def _():
            for d in range(DIRS):
                @pl.when((ways & (1 << d)) != 0)
                def _():
                    to = slot + shifts[d]
                    send(parts.at[slot], parts.at[to], send_sem.at[d], part_sem.at[to], targets[d])
        for d in range(DIRS):
            sent = sent + (((ways >> d) & 1) << (5 * d))
        return sent

    def unit(u, now, sent, before, scores, scores_before):
        word = pick(units, u)
        slot, end = word & 63, word >> 6
        sent = lax.fori_loop(now, end, step, sent)
        score(slot, slot & (PARTS - 1), scores)
        combine_back(before, scores_before)
        return end, sent, slot

    for p in range(PARTS):
        await_copy(give_kv.at[p], kv_sem.at[p])

    def attend_own():
        key = lax.broadcasted_iota(jnp.int32, (BLK, rows), 0)
        query = lax.broadcasted_iota(jnp.int32, (BLK, rows), 1) % tokens
        causal = jnp.where(key <= query, jnp.float32(0), jnp.float32(MASKED))
        biases = [[jnp.float32(0), jnp.float32(MASKED)], [bias_of(1, 1), jnp.float32(0)]]
        for p in range(PARTS):
            await_copy(qx.at[p], q_sem.at[p])
            put_queries(p, pl.ds(pl.multiple_of(other * rows, rows), rows), qx[p].astype(jnp.float32))
        score(0, 0, even)
        for p in range(PARTS):
            if p + 1 < PARTS:
                score(p + 1, p + 1, (even, odd)[(p + 1) % 2])
            combine(p, p, (even, odd)[p % 2], biases, causal)

    opening = of_place(OPEN)
    sent = lax.fori_loop(0, opening, step, jnp.int32(0))
    attend_own()

    def two_units(i, state):
        state = unit(2 * i, *state, even, odd)
        return unit(2 * i + 1, *state, odd, even)

    _, sent, before = lax.fori_loop(0, len(UNITS) // 2, two_units, (opening, sent, jnp.int32(256)))
    combine_back(before, odd)

    def result(p, r, side):
        at_rows = pl.ds(pl.multiple_of(side * rows + r * tokens, tokens), tokens)
        return (acc[p, pl.ds(0, HD), at_rows] / acc[p, pl.ds(HD, 1), at_rows]).T.astype(jnp.bfloat16)

    for p in range(PARTS):
        for r in range(group):
            give_out[p, pl.ds(r * tokens, tokens), :] = result(p, r, other)
        send(give_out.at[p], o_ref.at[core * PARTS + p], out_send, out_sem, pair)
    for p in range(PARTS):
        for r in range(group):
            o_ref[core * PARTS + p, pl.ds(r * tokens, tokens), :] = result(p, r, core)

    for d in range(DIRS):
        for n in range(1, MOST + 1):
            @pl.when(((sent >> (5 * d)) & 31) == n)
            def _():
                await_copy(parts.at[pl.ds(0, n)], send_sem.at[d])
    await_copy(give_kv, kv_send)
    await_copy(give_q, q_send)
    await_copy(give_out, out_send)
    await_copy(give_out, out_sem)


def on_device(queries, keys, values, doc_blocks):
    tokens, q_heads, _ = queries.shape
    kv_heads = keys.shape[1]
    group = q_heads // kv_heads
    rows = group * tokens
    bf16, f32 = jnp.bfloat16, jnp.float32
    anywhere = pl.BlockSpec(memory_space=pl.ANY)
    dma = pltpu.SemaphoreType.DMA
    by_head = pl.pallas_call(
        kernel,
        out_shape=jax.ShapeDtypeStruct((kv_heads, rows, HD), bf16),
        in_specs=[anywhere] * 4,
        out_specs=pl.BlockSpec(memory_space=pltpu.VMEM),
        scratch_shapes=[
            pltpu.VMEM(queries.shape, bf16),
            pltpu.VMEM(keys.shape, bf16),
            pltpu.VMEM(values.shape, bf16),
            pltpu.SMEM(doc_blocks.shape, jnp.int32),
            pltpu.VMEM(((THROUGH + 1) * PARTS, 4 * BLK, HD), bf16),
            pltpu.VMEM((PARTS, 2 * BLK, HD), bf16),
            pltpu.VMEM((PARTS, HD, rows), bf16),
            pltpu.VMEM((PARTS, rows, HD), bf16),
            pltpu.VMEM((PARTS, HD, rows), bf16),
            pltpu.VMEM((tokens * q_heads, HD), f32),
            pltpu.VMEM((tokens * kv_heads, HD), f32),
            pltpu.VMEM((tokens * kv_heads, HD), f32),
            pltpu.VMEM((PARTS, 2 * HD, 2 * rows), bf16),
            pltpu.VMEM((PARTS, HD + 16, 2 * rows), f32),
            pltpu.VMEM((PARTS, 8, 2 * rows), f32),
            pltpu.VMEM((2 * BLK, 2 * rows), f32),
            pltpu.VMEM((2 * BLK, 2 * rows), f32),
            dma((4,)),
            dma((DIRS,)),
            dma(((THROUGH + 1) * PARTS,)),
            dma,
            dma((PARTS,)),
            dma,
            dma((PARTS,)),
            dma,
            dma,
        ],
        compiler_params=pltpu.CompilerParams(
            collective_id=0, has_side_effects=True, vmem_limit_bytes=63 << 20
        ),
        name="attend",
    )(queries, keys, values, doc_blocks)
    by_head = by_head.reshape(q_heads, tokens, HD)
    return jnp.transpose(by_head, (1, 0, 2))


def solution(mesh):
    placed = P(("ctx", "dp"), None, None)
    return jax.shard_map(
        on_device,
        mesh=mesh,
        in_specs=(placed, placed, placed, P()),
        out_specs=placed,
        check_vma=False,
    )
```

```python
import jax
import jax.numpy as jnp
from jax import lax
from jax.experimental import pallas as pl
from jax.experimental.pallas import tpu as pltpu
from jax.sharding import PartitionSpec as P

STEPS = (
    (2113797, 2113793, 2138375, 2130183, 2138375, 2105602, 8438791, 8446981),
    (4202758, 4194564, 8388866, 8388865, 8438019, 8438016, 16786436, 8406016),
    (4235780, 4235783, 8438787, 25207814, 8389636, 8422407, 16820227, 3449862),
    (8446982, 8422406, 16820231, 16803841, 16836613, 16820227, 35202048, 5439626),
    (16819200, 16835589, 10520577, 8405254, 2099201, 8429830, 7660546, 1123332),
    (16803841, 16787461, 5506305, 5506307, 2147329, 8388871, 35217551, 5497767),
    (4194567, 29384966, 9547983, 35233929, 5555202, 1172134, 35234457, 1115137),
    (10520067, 8397316, 5529862, 2139145, 11661517, 10612939, 7652367, 5481376),
    (1364173, 35250598, 9523405, 35201702, 1155748, 1147559, 3678349, 3425283),
    (2105862, 4244482, 5554432, 8396938, 8417487, 2199757, 8430236, 4472974),
    (9760969, 35234212, 1167561, 5546250, 35201293, 5538819, 1139139, 8470683),
    (4251907, 1352193, 10601118, 1151179, 5505183, 5791881, 1614756, 1171878),
    (1315019, 13832393, 5537935, 2097822, 5808266, 8397065, 8397469, 4415644),
    (2098328, 1336717, 1278663, 1163938, 8429834, 1163920, 1114528, 3441695),
    (9560600, 1298635, 8618255, 9691845, 1147025, 2212517, 4391064, 4489367),
    (1613987, 8634918, 5513413, 1425666, 1630881, 1614887, 1328131, 8462494),
    (2220187, 1630607, 1245324, 1335489, 8528140, 1138847, 1269902, 1212833),
    (1164827, 1286305, 8585475, 1278495, 5521566, 8487584, 8495650, 1253926),
    (1343681, 8512037, 1122844, 12812582, 1581193, 5431589, 1237423, 1188884),
    (2211998, 1613986, 1581229, 1597609, 8462596, 1433741, 8478878, 4465059),
    (8503846, 13812104, 2408637, 1532076, 1163412, 2188311, 7643285, 8675504),
    (1630377, 1597633, 4563998, 4481321, 8470703, 4579480, 8560799, 3489942),
    (1228995, 1130680, 1392779, 1220769, 5472559, 11681955, 1196961, 1557022),
    (4514080, 4432026, 2179225, 2270344, 1114787, 4481173, 8536752, 3662871),
    (1401886, 1418250, 4400143, 9626177, 8618254, 1319048, 1212835, 4399533),
    (1278136, 1548686, 1425544, 9674943, 5546133, 8560900, 4481203, 8618173),
    (2384414, 8503853, 8487066, 4710702, 2392214, 4366490, 1147932, 1204649),
    (1147926, 1147070, 4538635, 9568444, 1180694, 1630346, 1556909, 1425968),
    (1564847, 4382871, 1540247, 2401432, 1237169, 8659205, 8553011, 3572753),
    (8618543, 1434636, 1228948, 1376792, 8577329, 1409171, 3498423, 4481178),
    (1532296, 1212553, 8462634, 1228943, 1139354, 1425953, 8454335, 8569013),
    (3334297, 8462895, 1507866, 1499404, 8560809, 2204691, 1229749, 1147331),
    (8454658, 3236278, 1269928, 9757224, 1286401, 1499804, 8609974, 1614403),
    (1212846, 12746907, 4760601, 5742888, 1425578, 4407473, 1409458, 1156120),
    (3253273, 3293610, 1401022, 2375835, 2171933, 2163740, 8504007, 1434039),
    (5546174, 4481209, 3276957, 1441933, 5735065, 1286302, 5734841, 1221640),
    (8495241, 3523610, 4686850, 1557019, 8519826, 1458707, 8585370, 5825212),
    (13770934, 1499559, 3399855, 2490521, 1376520, 2499613, 5669001, 1180691),
    (1540235, 8610330, 8642706, 4587704, 1491091, 5677209, 1188029, 1409457),
    (9609890, 1220780, 4653494, 9601171, 2434073, 2121910, 1384872, 8602161),
    (9585064, 8536208, 8536236, 2384050, 1499803, 1229854, 1180347, 1515702),
    (1515935, 1188777, 4341909, 1630776, 2113714, 4399297, 1450170, 1458363),
    (9593021, 8528032, 8675497, 1197210, 1401891, 2384045, 1130670, 1138872),
    (1474989, 3375284, 8528017, 1491250, 1245365, 1188889, 1392824, 1401025),
    (1450397, 8618165, 5669049, 4776218, 8585506, 4726932, 147, 1466536),
    (9650352, 1401018, 8601762, 1433739, 1548461, 4604083, 0, 1523858),
    (1130677, 8544403, 1204927, 1417396, 2187431, 1376522, 0, 0),
    (1458337, 1302715, 8609968, 1450129, 5760026, 1540659, 0, 0),
    (1409168, 1458344, 5653523, 1515706, 1556656, 1269936, 0, 0),
    (1499315, 1441945, 1597607, 1343658, 1475611, 1393341, 0, 0),
    (1523882, 1564849, 1450165, 1482923, 1409209, 5726392, 0, 0),
    (0, 1466556, 1523877, 179, 1507523, 1556651, 0, 0),
    (0, 0, 1532087, 0, 1523891, 1474746, 0, 0),
    (0, 0, 179, 0, 187, 1515682, 0, 0),
    (0, 0, 0, 0, 0, 1384639, 0, 0),
)
UNITS = (
    (1427, 1554, 1607, 1890, 1698, 1107, 1043, 900),
    (2082, 2211, 1763, 1935, 1926, 1569, 1184, 1491),
    (2311, 2513, 2018, 2144, 2064, 1799, 1377, 1543),
    (2464, 2658, 2128, 2257, 2211, 1874, 1570, 1742),
    (2851, 2784, 2310, 2593, 2255, 2082, 1678, 1810),
    (2913, 2849, 2592, 2896, 2464, 2502, 1868, 1999),
    (4044, 3271, 2885, 3012, 2695, 3140, 2119, 2128),
    (4235, 3590, 3020, 3342, 3025, 3216, 2706, 2316),
    (4311, 3659, 3268, 3860, 3076, 3525, 2767, 2513),
    (4486, 3908, 3742, 3911, 3274, 3619, 2896, 2763),
    (4575, 4229, 3851, 4043, 3410, 3785, 3153, 3103),
    (4626, 4301, 4237, 4243, 3592, 3991, 3210, 3789),
    (4740, 4572, 4501, 4382, 3723, 4559, 3462, 3930),
    (5073, 4759, 4558, 4550, 3973, 4750, 3935, 4065),
    (5130, 4819, 4823, 4767, 4238, 4940, 4107, 4258),
    (5204, 5019, 4879, 4876, 4375, 5083, 4187, 4358),
    (5327, 5078, 5206, 5130, 4884, 5259, 4313, 4503),
    (5404, 5130, 5322, 5411, 5001, 5472, 4374, 4618),
    (5470, 5384, 5460, 5453, 5197, 5462, 4515, 4702),
    (5513, 5456, 5576, 5641, 5339, 5640, 4685, 4835),
    (5710, 5646, 5724, 5659, 5525, 5834, 4804, 4872),
    (5848, 5722, 5841, 5829, 5644, 5913, 4890, 4952),
    (5901, 5909, 5983, 5911, 5918, 6232, 4958, 5142),
    (5978, 5961, 6025, 6038, 5971, 6285, 5140, 5211),
    (6021, 6109, 6355, 6088, 6232, 6430, 5256, 5468),
    (6096, 6159, 6433, 6168, 6303, 6613, 5341, 5509),
    (6216, 6228, 6490, 6301, 6426, 6749, 5400, 5600),
    (6294, 6348, 6552, 6300, 6550, 6810, 5463, 5653),
    (6361, 6488, 6610, 6418, 6625, 6929, 5509, 5716),
    (6427, 6559, 6747, 6485, 6684, 6940, 5596, 5785),
    (6485, 6622, 6813, 6554, 6745, 7007, 5653, 5833),
    (6557, 6681, 6873, 6617, 6877, 7060, 5705, 5917),
)
OPEN = (16, 16, 11, 11, 13, 12, 7, 5)
MOST = 23
PARTS = 4
BACK = 8
THROUGH = 9
DIRS = 5
BLK = 128
HD = 128
LOG2E = 1.4426950408889634
MASKED = -1e30
MESH = pl.DeviceIdType.MESH


def kernel(
    q_hbm, k_hbm, v_hbm, docs_hbm, o_ref,
    q_in, k_in, v_in, docs, parts, give_kv, give_q, give_out, qx, qf, kf, vf, qs, acc, top, even, odd,
    load_sem, send_sem, part_sem, kv_send, kv_sem, q_send, q_sem, out_send, out_sem,
):
    tokens, q_heads, _ = q_in.shape
    kv_heads = k_in.shape[1]
    group = q_heads // kv_heads
    rows = group * tokens
    dp = lax.axis_index("dp")
    z = lax.axis_index("ctx")
    planes = lax.axis_size("ctx")
    x, y, core = dp // 8, (dp // 2) % 4, dp % 2
    chip = dp // 2
    other = 1 - core

    def one_if(condition):
        return jnp.where(condition, jnp.int32(1), jnp.int32(0))

    def at(to_x, to_y, to_z, to_core):
        return ((to_x % 4) * 8 + (to_y % 4) * 2 + to_core, to_z)

    loads = [
        pltpu.make_async_copy(src, dst, load_sem.at[i])
        for i, (src, dst) in enumerate(((k_hbm, k_in), (v_hbm, v_in), (q_hbm, q_in), (docs_hbm, docs)))
    ]
    for load in loads:
        load.start()

    over_ahead = one_if(x == 3)
    over_beyond = one_if((x == 1) | (x == 2))
    has_ahead = z + over_ahead < planes
    has_behind = z - one_if(x == 0) >= 0
    has_beyond = z + over_beyond < planes
    has_beyond_from = z - one_if(x <= 1) >= 0
    has_through = z + one_if(x >= 2) < planes
    pair = at(x, y, z, other)
    up = at(x, y + 1, z, core)
    down = at(x, y + 3, z, core)
    ahead = at(x + 1, y, z + over_ahead, core)
    through = at(x + 3, y, z, core)

    last_here = PARTS * jnp.where(z > 0, jnp.int32(BACK), jnp.minimum(chip, BACK)) + PARTS - 1

    def clear(slot, c):
        parts[slot] = jnp.zeros((2 * BLK, HD), jnp.bfloat16)
        return c
    lax.fori_loop(2 * (last_here + 1), 2 * (BACK + 1) * PARTS, clear, 0)
    for p in range(PARTS):
        clear(2 * (BACK * PARTS + p), 0)

    barrier = pltpu.get_barrier_semaphore()

    def greet(device):
        pl.semaphore_signal(barrier, inc=1, device_id=device, device_id_type=MESH)

    for friend in (pair, up, down, through, at(x + 1, y, z, core)):
        greet(friend)
    maybe = (
        (has_ahead, ahead),
        (has_behind, at(x + 3, y, z - one_if(x == 0), core)),
        (has_beyond, at(x + 3, y, z + over_beyond, core)),
        (has_beyond_from, at(x + 1, y, z - one_if(x <= 1), core)),
    )
    greeted = jnp.int32(5)
    for there, friend in maybe:
        greeted = greeted + one_if(there)
        pl.when(there)(lambda friend=friend: greet(friend))

    def of_place(entry):
        pairs = [jnp.where(core == 0, jnp.int32(entry[2 * i]), jnp.int32(entry[2 * i + 1])) for i in range(4)]
        return jnp.where(y < 2, jnp.where(y == 0, pairs[0], pairs[1]), jnp.where(y == 2, pairs[2], pairs[3]))

    steps = [of_place(entry) for entry in STEPS]
    units = [of_place(entry) for entry in UNITS]

    def pick(values, index):
        while len(values) > 1:
            low = (index & 1) == 0
            values = [
                jnp.where(low, values[i], values[i + 1]) if i + 1 < len(values) else values[i]
                for i in range(0, len(values), 2)
            ]
            index = index >> 1
        return values[0]

    loads[0].wait()
    kf[...] = k_in[...].astype(jnp.float32).reshape(tokens * kv_heads, HD)
    loads[1].wait()
    vf[...] = v_in[...].astype(jnp.float32).reshape(tokens * kv_heads, HD)
    for p in range(PARTS):
        head = pl.ds(other * PARTS + p, tokens, stride=kv_heads)
        give_kv[p, pl.ds(0, BLK), :] = kf[head, :].astype(jnp.bfloat16)
        give_kv[p, pl.ds(BLK, BLK), :] = vf[head, :].T.astype(jnp.bfloat16)
    for p in range(PARTS):
        head = pl.ds(core * PARTS + p, tokens, stride=kv_heads)
        parts[2 * p + core, pl.ds(0, BLK), :] = kf[head, :].astype(jnp.bfloat16)
        parts[2 * p + core, pl.ds(BLK, BLK), :] = vf[head, :].T.astype(jnp.bfloat16)

    pl.semaphore_wait(barrier, greeted)

    def send(src, dst, sem, landed, device):
        pltpu.make_async_remote_copy(
            src_ref=src, dst_ref=dst, send_sem=sem, recv_sem=landed, device_id=device, device_id_type=MESH
        ).start()

    def await_copy(ref, sem):
        pltpu.make_async_copy(ref, ref, sem).wait()

    for p in range(PARTS):
        send(give_kv.at[p], parts.at[2 * p + core], kv_send, kv_sem.at[p], pair)

    loads[2].wait()
    qf[...] = q_in[...].astype(jnp.float32).reshape(tokens * q_heads, HD)

    def queries_of(p, r, side):
        return qf[pl.ds((side * PARTS + p) * group + r, tokens, stride=q_heads), :].T

    for p in range(PARTS):
        for r in range(group):
            give_q[p, :, pl.ds(r * tokens, tokens)] = queries_of(p, r, other).astype(jnp.bfloat16)
        send(give_q.at[p], qx.at[p], q_send, q_sem.at[p], pair)

    scale = LOG2E * HD**-0.5

    def put_queries(p, at_rows, value):
        scaled = value * scale
        high = scaled.astype(jnp.bfloat16)
        qs[p, pl.ds(0, HD), at_rows] = high
        qs[p, pl.ds(HD, HD), at_rows] = (scaled - high.astype(jnp.float32)).astype(jnp.bfloat16)

    for p in range(PARTS):
        for r in range(group):
            put_queries(p, pl.ds(pl.multiple_of(core * rows + r * tokens, tokens), tokens), queries_of(p, r, core))

    loads[3].wait()
    reach = []
    for b in range(2):
        block = (z * 16 + chip) * 2 + b
        end = jnp.int32(0)
        start = jnp.int32(0)
        for i in range(docs.shape[0]):
            end = end + docs[i]
            start = jnp.where(end <= block, end, start)
        reach.append(block - start)

    def bias_of(back, b):
        return jnp.where(back <= reach[b], jnp.float32(0), jnp.float32(MASKED))

    ones = jnp.ones((16, 2 * BLK), jnp.bfloat16)

    def score(slot, p, into):
        keys = jnp.concatenate([parts[2 * slot, pl.ds(0, BLK), :], parts[2 * slot + 1, pl.ds(0, BLK), :]], axis=0)
        keys = jnp.concatenate([keys, keys], axis=1)
        for b in range(2):
            at_rows = pl.ds(b * rows, rows)
            into[:, at_rows] = jnp.dot(keys, qs[p, :, at_rows], preferred_element_type=jnp.float32)

    def combine(slot, p, scores, biases, causal=None):
        values = jnp.concatenate([parts[2 * slot, pl.ds(BLK, BLK), :], parts[2 * slot + 1, pl.ds(BLK, BLK), :]], axis=1)
        values = jnp.concatenate([values, ones], axis=0)
        for b in range(2):
            at_rows = pl.ds(b * rows, rows)
            halves = [scores[pl.ds(h * BLK, BLK), at_rows] for h in range(2)]
            if causal is not None:
                halves[b] = halves[b] + causal
            peaks = [jnp.max(halves[h], axis=0, keepdims=True) + biases[b][h] for h in range(2)]
            new_top = jnp.maximum(peaks[0], peaks[1])
            if causal is None:
                old_top = top[p, pl.ds(0, 1), at_rows]
                new_top = jnp.maximum(old_top, new_top)
            weights = [jnp.exp2(halves[h] - (new_top - biases[b][h])).astype(jnp.bfloat16) for h in range(2)]
            summed = jnp.dot(values, jnp.concatenate(weights, axis=0), preferred_element_type=jnp.float32)
            if causal is None:
                acc[p, :, at_rows] = acc[p, :, at_rows] * jnp.exp2(old_top - new_top) + summed
            else:
                acc[p, :, at_rows] = summed
            top[p, pl.ds(0, 1), at_rows] = new_top

    def combine_back(code, scores):
        k, p = code >> 2, code & (PARTS - 1)
        biases = [[bias_of(2 * k + b - h, b) for h in range(2)] for b in range(2)]
        combine(code & 63, p, scores, biases)

    shifts = (
        PARTS * jnp.where(y == 3, jnp.int32(-3), jnp.int32(1)),
        PARTS * jnp.where(y == 0, jnp.int32(3), jnp.int32(-1)),
        4 * PARTS,
        THROUGH * PARTS,
        (BACK - THROUGH) * PARTS,
    )
    targets = (up, down, ahead, through, at(x + 3, y, z + over_beyond, core))
    open_ways = 3 + 4 * one_if(has_ahead) + 8 * one_if(has_through) + 16 * one_if(has_beyond)

    def step(s, sent):
        word = pick(steps, s >> 1) >> (13 * (s & 1))
        block = word & 127
        slot = block >> 1
        here = (slot <= last_here) | ((slot >= THROUGH * PARTS) & has_beyond)
        ways = jnp.where(here, (word >> 8) & open_ways, 0)

        @pl.when(here & ((word & 128) != 0))
        def _():
            await_copy(parts.at[block], part_sem.at[block])

        @pl.when(ways != 0)
        def _():
            for d in range(DIRS):
                @pl.when((ways & (1 << d)) != 0)
                def _():
                    to = block + 2 * shifts[d]
                    send(parts.at[block], parts.at[to], send_sem.at[d], part_sem.at[to], targets[d])
        for d in range(DIRS):
            sent = sent + (((ways >> d) & 1) << (6 * d))
        return sent

    def unit(u, now, sent, before, scores, scores_before):
        word = pick(units, u)
        slot, end = word & 63, word >> 6
        sent = lax.fori_loop(now, end, step, sent)
        score(slot, slot & (PARTS - 1), scores)
        combine_back(before, scores_before)
        return end, sent, slot

    for p in range(PARTS):
        await_copy(give_kv.at[p], kv_sem.at[p])

    def attend_own():
        key = lax.broadcasted_iota(jnp.int32, (BLK, rows), 0)
        query = lax.broadcasted_iota(jnp.int32, (BLK, rows), 1) % tokens
        causal = jnp.where(key <= query, jnp.float32(0), jnp.float32(MASKED))
        biases = [[jnp.float32(0), jnp.float32(MASKED)], [bias_of(1, 1), jnp.float32(0)]]
        for p in range(PARTS):
            await_copy(qx.at[p], q_sem.at[p])
            put_queries(p, pl.ds(pl.multiple_of(other * rows, rows), rows), qx[p].astype(jnp.float32))
        score(0, 0, even)
        for p in range(PARTS):
            if p + 1 < PARTS:
                score(p + 1, p + 1, (even, odd)[(p + 1) % 2])
            combine(p, p, (even, odd)[p % 2], biases, causal)

    opening = of_place(OPEN)
    sent = lax.fori_loop(0, opening, step, jnp.int32(0))
    attend_own()

    def two_units(i, state):
        state = unit(2 * i, *state, even, odd)
        return unit(2 * i + 1, *state, odd, even)

    _, sent, before = lax.fori_loop(0, len(UNITS) // 2, two_units, (opening, sent, jnp.int32(256)))
    combine_back(before, odd)

    def result(p, r, side):
        at_rows = pl.ds(pl.multiple_of(side * rows + r * tokens, tokens), tokens)
        return (acc[p, pl.ds(0, HD), at_rows] / acc[p, pl.ds(HD, 1), at_rows]).T.astype(jnp.bfloat16)

    for p in range(PARTS):
        for r in range(group):
            give_out[p, :, pl.ds(r * HD, HD)] = result(p, r, other)
        send(give_out.at[p], o_ref.at[:, pl.ds(pl.multiple_of((core * PARTS + p) * rows, rows), rows)], out_send, out_sem, pair)
    for p in range(PARTS):
        for r in range(group):
            place = pl.ds(pl.multiple_of((core * PARTS + p) * rows + r * HD, HD), HD)
            o_ref[:, place] = result(p, r, core)

    for d in range(DIRS):
        for n in range(1, MOST + 1):
            @pl.when(((sent >> (6 * d)) & 63) == n)
            def _():
                await_copy(parts.at[pl.ds(0, n)], send_sem.at[d])
    await_copy(give_kv, kv_send)
    await_copy(give_q, q_send)
    await_copy(give_out, out_send)
    await_copy(give_out, out_sem)


def on_device(queries, keys, values, doc_blocks):
    tokens, q_heads, _ = queries.shape
    kv_heads = keys.shape[1]
    group = q_heads // kv_heads
    rows = group * tokens
    bf16, f32 = jnp.bfloat16, jnp.float32
    anywhere = pl.BlockSpec(memory_space=pl.ANY)
    dma = pltpu.SemaphoreType.DMA
    flat = pl.pallas_call(
        kernel,
        out_shape=jax.ShapeDtypeStruct((tokens, q_heads * HD), bf16),
        in_specs=[anywhere] * 4,
        out_specs=pl.BlockSpec(memory_space=pltpu.VMEM),
        scratch_shapes=[
            pltpu.VMEM(queries.shape, bf16),
            pltpu.VMEM(keys.shape, bf16),
            pltpu.VMEM(values.shape, bf16),
            pltpu.SMEM(doc_blocks.shape, jnp.int32),
            pltpu.VMEM(((THROUGH + 1) * PARTS * 2, 2 * BLK, HD), bf16),
            pltpu.VMEM((PARTS, 2 * BLK, HD), bf16),
            pltpu.VMEM((PARTS, HD, rows), bf16),
            pltpu.VMEM((PARTS, tokens, group * HD), bf16),
            pltpu.VMEM((PARTS, HD, rows), bf16),
            pltpu.VMEM((tokens * q_heads, HD), f32),
            pltpu.VMEM((tokens * kv_heads, HD), f32),
            pltpu.VMEM((tokens * kv_heads, HD), f32),
            pltpu.VMEM((PARTS, 2 * HD, 2 * rows), bf16),
            pltpu.VMEM((PARTS, HD + 16, 2 * rows), f32),
            pltpu.VMEM((PARTS, 8, 2 * rows), f32),
            pltpu.VMEM((2 * BLK, 2 * rows), f32),
            pltpu.VMEM((2 * BLK, 2 * rows), f32),
            dma((4,)),
            dma((DIRS,)),
            dma(((THROUGH + 1) * PARTS * 2,)),
            dma,
            dma((PARTS,)),
            dma,
            dma((PARTS,)),
            dma,
            dma,
        ],
        compiler_params=pltpu.CompilerParams(
            collective_id=0, has_side_effects=True, vmem_limit_bytes=63 << 20
        ),
        name="attend",
    )(queries, keys, values, doc_blocks)
    return flat.reshape(queries.shape)


def solution(mesh):
    placed = P(("ctx", "dp"), None, None)
    return jax.shard_map(
        on_device,
        mesh=mesh,
        in_specs=(placed, placed, placed, P()),
        out_specs=placed,
        check_vma=False,
    )
```

```python
import jax
import jax.numpy as jnp
from jax import lax
from jax.experimental import pallas as pl
from jax.experimental.pallas import tpu as pltpu
from jax.sharding import PartitionSpec as P

STEPS = (
    (2113797, 2113793, 2138375, 2130183, 2138375, 2105602, 8438791, 8446981),
    (4202758, 4194564, 8388866, 8388865, 8438019, 8438016, 16786436, 8406016),
    (4235780, 4235783, 8438787, 25207814, 8389636, 8422407, 16820227, 3449862),
    (8446982, 8422406, 16820231, 16803841, 16836613, 16820227, 35202048, 5439626),
    (16819200, 16835589, 10520577, 8405254, 2099201, 8429830, 7660546, 1123332),
    (16803841, 16787461, 5506305, 5506307, 2147329, 8388871, 35217551, 5497767),
    (4194567, 29384966, 9547983, 35233929, 5555202, 1172134, 35234457, 1115137),
    (10520067, 8397316, 5529862, 2139145, 11661517, 10612939, 7652367, 5481376),
    (1364173, 35250598, 9523405, 35201702, 1155748, 1147559, 3678349, 3425283),
    (2105862, 4244482, 5554432, 8396938, 8417487, 2199757, 8430236, 4472974),
    (9760969, 35234212, 1167561, 5546250, 35201293, 5538819, 1139139, 8470683),
    (4251907, 1352193, 10601118, 1151179, 5505183, 5791881, 1614756, 1171878),
    (1315019, 13832393, 5537935, 2097822, 5808266, 8397065, 8397469, 4415644),
    (2098328, 1336717, 1278663, 1163938, 8429834, 1163920, 1114528, 3441695),
    (9560600, 1298635, 8618255, 9691845, 1147025, 2212517, 4391064, 4489367),
    (1613987, 8634918, 5513413, 1425666, 1630881, 1614887, 1328131, 8462494),
    (2220187, 1630607, 1245324, 1335489, 8528140, 1138847, 1269902, 1212833),
    (1164827, 1286305, 8585475, 1278495, 5521566, 8487584, 8495650, 1253926),
    (1343681, 8512037, 1122844, 12812582, 1581193, 5431589, 1237423, 1188884),
    (2211998, 1613986, 1581229, 1597609, 8462596, 1433741, 8478878, 4465059),
    (8503846, 13812104, 2408637, 1532076, 1163412, 2188311, 7643285, 8675504),
    (1630377, 1597633, 4563998, 4481321, 8470703, 4579480, 8560799, 3489942),
    (1228995, 1130680, 1392779, 1220769, 5472559, 11681955, 1196961, 1557022),
    (4514080, 4432026, 2179225, 2270344, 1114787, 4481173, 8536752, 3662871),
    (1401886, 1418250, 4400143, 9626177, 8618254, 1319048, 1212835, 4399533),
    (1278136, 1548686, 1425544, 9674943, 5546133, 8560900, 4481203, 8618173),
    (2384414, 8503853, 8487066, 4710702, 2392214, 4366490, 1147932, 1204649),
    (1147926, 1147070, 4538635, 9568444, 1180694, 1630346, 1556909, 1425968),
    (1564847, 4382871, 1540247, 2401432, 1237169, 8659205, 8553011, 3572753),
    (8618543, 1434636, 1228948, 1376792, 8577329, 1409171, 3498423, 4481178),
    (1532296, 1212553, 8462634, 1228943, 1139354, 1425953, 8454335, 8569013),
    (3334297, 8462895, 1507866, 1499404, 8560809, 2204691, 1229749, 1147331),
    (8454658, 3236278, 1269928, 9757224, 1286401, 1499804, 8609974, 1614403),
    (1212846, 12746907, 4760601, 5742888, 1425578, 4407473, 1409458, 1156120),
    (3253273, 3293610, 1401022, 2375835, 2171933, 2163740, 8504007, 1434039),
    (5546174, 4481209, 3276957, 1441933, 5735065, 1286302, 5734841, 1221640),
    (8495241, 3523610, 4686850, 1557019, 8519826, 1458707, 8585370, 5825212),
    (13770934, 1499559, 3399855, 2490521, 1376520, 2499613, 5669001, 1180691),
    (1540235, 8610330, 8642706, 4587704, 1491091, 5677209, 1188029, 1409457),
    (9609890, 1220780, 4653494, 9601171, 2434073, 2121910, 1384872, 8602161),
    (9585064, 8536208, 8536236, 2384050, 1499803, 1229854, 1180347, 1515702),
    (1515935, 1188777, 4341909, 1630776, 2113714, 4399297, 1450170, 1458363),
    (9593021, 8528032, 8675497, 1197210, 1401891, 2384045, 1130670, 1138872),
    (1474989, 3375284, 8528017, 1491250, 1245365, 1188889, 1392824, 1401025),
    (1450397, 8618165, 5669049, 4776218, 8585506, 4726932, 147, 1466536),
    (9650352, 1401018, 8601762, 1433739, 1548461, 4604083, 0, 1523858),
    (1130677, 8544403, 1204927, 1417396, 2187431, 1376522, 0, 0),
    (1458337, 1302715, 8609968, 1450129, 5760026, 1540659, 0, 0),
    (1409168, 1458344, 5653523, 1515706, 1556656, 1269936, 0, 0),
    (1499315, 1441945, 1597607, 1343658, 1475611, 1393341, 0, 0),
    (1523882, 1564849, 1450165, 1482923, 1409209, 5726392, 0, 0),
    (0, 1466556, 1523877, 179, 1507523, 1556651, 0, 0),
    (0, 0, 1532087, 0, 1523891, 1474746, 0, 0),
    (0, 0, 179, 0, 187, 1515682, 0, 0),
    (0, 0, 0, 0, 0, 1384639, 0, 0),
)
UNITS = (
    (1427, 1554, 1607, 1890, 1698, 1107, 1043, 900),
    (2082, 2211, 1763, 1935, 1926, 1569, 1184, 1491),
    (2311, 2513, 2018, 2144, 2064, 1799, 1377, 1543),
    (2464, 2658, 2128, 2257, 2211, 1874, 1570, 1742),
    (2851, 2784, 2310, 2593, 2255, 2082, 1678, 1810),
    (2913, 2849, 2592, 2896, 2464, 2502, 1868, 1999),
    (4044, 3271, 2885, 3012, 2695, 3140, 2119, 2128),
    (4235, 3590, 3020, 3342, 3025, 3216, 2706, 2316),
    (4311, 3659, 3268, 3860, 3076, 3525, 2767, 2513),
    (4486, 3908, 3742, 3911, 3274, 3619, 2896, 2763),
    (4575, 4229, 3851, 4043, 3410, 3785, 3153, 3103),
    (4626, 4301, 4237, 4243, 3592, 3991, 3210, 3789),
    (4740, 4572, 4501, 4382, 3723, 4559, 3462, 3930),
    (5073, 4759, 4558, 4550, 3973, 4750, 3935, 4065),
    (5130, 4819, 4823, 4767, 4238, 4940, 4107, 4258),
    (5204, 5019, 4879, 4876, 4375, 5083, 4187, 4358),
    (5327, 5078, 5206, 5130, 4884, 5259, 4313, 4503),
    (5404, 5130, 5322, 5411, 5001, 5472, 4374, 4618),
    (5470, 5384, 5460, 5453, 5197, 5462, 4515, 4702),
    (5513, 5456, 5576, 5641, 5339, 5640, 4685, 4835),
    (5710, 5646, 5724, 5659, 5525, 5834, 4804, 4872),
    (5848, 5722, 5841, 5829, 5644, 5913, 4890, 4952),
    (5901, 5909, 5983, 5911, 5918, 6232, 4958, 5142),
    (5978, 5961, 6025, 6038, 5971, 6285, 5140, 5211),
    (6021, 6109, 6355, 6088, 6232, 6430, 5256, 5468),
    (6096, 6159, 6433, 6168, 6303, 6613, 5341, 5509),
    (6216, 6228, 6490, 6301, 6426, 6749, 5400, 5600),
    (6294, 6348, 6552, 6300, 6550, 6810, 5463, 5653),
    (6361, 6488, 6610, 6418, 6625, 6929, 5509, 5716),
    (6427, 6559, 6747, 6485, 6684, 6940, 5596, 5785),
    (6485, 6622, 6813, 6554, 6745, 7007, 5653, 5833),
    (6557, 6681, 6873, 6617, 6877, 7060, 5705, 5917),
)
OPEN = (16, 16, 11, 11, 13, 12, 7, 5)
MOST = 23
PARTS = 4
BACK = 8
THROUGH = 9
DIRS = 5
BLK = 128
HD = 128
LOG2E = 1.4426950408889634
MASKED = -1e30
MESH = pl.DeviceIdType.MESH


def kernel(
    q_hbm, k_hbm, v_hbm, docs_hbm, o_ref,
    q_in, k_in, v_in, docs, parts, give_kv, give_q, give_out, qx, qf, kf, vf, qs, acc, top, even, odd,
    load_sem, send_sem, part_sem, kv_send, kv_sem, q_send, q_sem, out_send, out_sem,
):
    tokens, q_heads, _ = q_in.shape
    kv_heads = k_in.shape[1]
    group = q_heads // kv_heads
    rows = group * tokens
    dp = lax.axis_index("dp")
    z = lax.axis_index("ctx")
    planes = lax.axis_size("ctx")
    x, y, core = dp // 8, (dp // 2) % 4, dp % 2
    chip = dp // 2
    other = 1 - core

    def one_if(condition):
        return jnp.where(condition, jnp.int32(1), jnp.int32(0))

    def at(to_x, to_y, to_z, to_core):
        return ((to_x % 4) * 8 + (to_y % 4) * 2 + to_core, to_z)

    loads = [
        pltpu.make_async_copy(src, dst, load_sem.at[i])
        for i, (src, dst) in enumerate(((k_hbm, k_in), (v_hbm, v_in), (q_hbm, q_in), (docs_hbm, docs)))
    ]
    for load in loads:
        load.start()

    over_ahead = one_if(x == 3)
    over_beyond = one_if((x == 1) | (x == 2))
    has_ahead = z + over_ahead < planes
    has_behind = z - one_if(x == 0) >= 0
    has_beyond = z + over_beyond < planes
    has_beyond_from = z - one_if(x <= 1) >= 0
    has_through = z + one_if(x >= 2) < planes
    pair = at(x, y, z, other)
    up = at(x, y + 1, z, core)
    down = at(x, y + 3, z, core)
    ahead = at(x + 1, y, z + over_ahead, core)
    through = at(x + 3, y, z, core)

    last_here = PARTS * jnp.where(z > 0, jnp.int32(BACK), jnp.minimum(chip, BACK)) + PARTS - 1

    def clear(slot, c):
        parts[slot] = jnp.zeros((2 * BLK, HD), jnp.bfloat16)
        return c
    lax.fori_loop(2 * (last_here + 1), 2 * (BACK + 1) * PARTS, clear, 0)
    for p in range(PARTS):
        clear(2 * (BACK * PARTS + p), 0)

    barrier = pltpu.get_barrier_semaphore()

    def greet(device):
        pl.semaphore_signal(barrier, inc=1, device_id=device, device_id_type=MESH)

    for friend in (pair, up, down, through, at(x + 1, y, z, core)):
        greet(friend)
    maybe = (
        (has_ahead, ahead),
        (has_behind, at(x + 3, y, z - one_if(x == 0), core)),
        (has_beyond, at(x + 3, y, z + over_beyond, core)),
        (has_beyond_from, at(x + 1, y, z - one_if(x <= 1), core)),
    )
    greeted = jnp.int32(5)
    for there, friend in maybe:
        greeted = greeted + one_if(there)
        pl.when(there)(lambda friend=friend: greet(friend))

    def of_place(entry):
        pairs = [jnp.where(core == 0, jnp.int32(entry[2 * i]), jnp.int32(entry[2 * i + 1])) for i in range(4)]
        return jnp.where(y < 2, jnp.where(y == 0, pairs[0], pairs[1]), jnp.where(y == 2, pairs[2], pairs[3]))

    steps = [of_place(entry) for entry in STEPS]
    units = [of_place(entry) for entry in UNITS]

    def pick(values, index):
        while len(values) > 1:
            low = (index & 1) == 0
            values = [
                jnp.where(low, values[i], values[i + 1]) if i + 1 < len(values) else values[i]
                for i in range(0, len(values), 2)
            ]
            index = index >> 1
        return values[0]

    loads[0].wait()
    kf[...] = k_in[...].astype(jnp.float32).reshape(tokens * kv_heads, HD)
    loads[1].wait()
    vf[...] = v_in[...].astype(jnp.float32).reshape(tokens * kv_heads, HD)
    for p in range(PARTS):
        head = pl.ds(other * PARTS + p, tokens, stride=kv_heads)
        give_kv[p, pl.ds(0, BLK), :] = kf[head, :].astype(jnp.bfloat16)
        give_kv[p, pl.ds(BLK, BLK), :] = vf[head, :].T.astype(jnp.bfloat16)
    for p in range(PARTS):
        head = pl.ds(core * PARTS + p, tokens, stride=kv_heads)
        parts[2 * p + core, pl.ds(0, BLK), :] = kf[head, :].astype(jnp.bfloat16)
        parts[2 * p + core, pl.ds(BLK, BLK), :] = vf[head, :].T.astype(jnp.bfloat16)

    pl.semaphore_wait(barrier, greeted)

    def send(src, dst, sem, landed, device):
        pltpu.make_async_remote_copy(
            src_ref=src, dst_ref=dst, send_sem=sem, recv_sem=landed, device_id=device, device_id_type=MESH
        ).start()

    def await_copy(ref, sem):
        pltpu.make_async_copy(ref, ref, sem).wait()

    for p in range(PARTS):
        send(give_kv.at[p], parts.at[2 * p + core], kv_send, kv_sem.at[p], pair)

    loads[3].wait()
    reach = []
    for b in range(2):
        block = (z * 16 + chip) * 2 + b
        end = jnp.int32(0)
        start = jnp.int32(0)
        for i in range(docs.shape[0]):
            end = end + docs[i]
            start = jnp.where(end <= block, end, start)
        reach.append(block - start)

    def bias_of(back, b):
        return jnp.where(back <= reach[b], jnp.float32(0), jnp.float32(MASKED))

    ones = jnp.ones((16, 2 * BLK), jnp.bfloat16)

    def score(slot, p, into):
        keys = jnp.concatenate([parts[2 * slot, pl.ds(0, BLK), :], parts[2 * slot + 1, pl.ds(0, BLK), :]], axis=0)
        keys = jnp.concatenate([keys, keys], axis=1)
        for b in range(2):
            at_rows = pl.ds(b * rows, rows)
            into[:, at_rows] = jnp.dot(keys, qs[p, :, at_rows], preferred_element_type=jnp.float32)

    def combine(slot, p, scores, biases, causal=None):
        values = jnp.concatenate([parts[2 * slot, pl.ds(BLK, BLK), :], parts[2 * slot + 1, pl.ds(BLK, BLK), :]], axis=1)
        values = jnp.concatenate([values, ones], axis=0)
        for b in range(2):
            at_rows = pl.ds(b * rows, rows)
            halves = [scores[pl.ds(h * BLK, BLK), at_rows] for h in range(2)]
            if causal is not None:
                halves[b] = halves[b] + causal
            peaks = [jnp.max(halves[h], axis=0, keepdims=True) + biases[b][h] for h in range(2)]
            new_top = jnp.maximum(peaks[0], peaks[1])
            if causal is None:
                old_top = top[p, pl.ds(0, 1), at_rows]
                new_top = jnp.maximum(old_top, new_top)
            weights = [jnp.exp2(halves[h] - (new_top - biases[b][h])).astype(jnp.bfloat16) for h in range(2)]
            summed = jnp.dot(values, jnp.concatenate(weights, axis=0), preferred_element_type=jnp.float32)
            if causal is None:
                acc[p, :, at_rows] = acc[p, :, at_rows] * jnp.exp2(old_top - new_top) + summed
            else:
                acc[p, :, at_rows] = summed
            top[p, pl.ds(0, 1), at_rows] = new_top

    def combine_back(code, scores):
        k, p = code >> 2, code & (PARTS - 1)
        biases = [[bias_of(2 * k + b - h, b) for h in range(2)] for b in range(2)]
        combine(code & 63, p, scores, biases)

    shifts = (
        PARTS * jnp.where(y == 3, jnp.int32(-3), jnp.int32(1)),
        PARTS * jnp.where(y == 0, jnp.int32(3), jnp.int32(-1)),
        4 * PARTS,
        THROUGH * PARTS,
        (BACK - THROUGH) * PARTS,
    )
    targets = (up, down, ahead, through, at(x + 3, y, z + over_beyond, core))
    open_ways = 3 + 4 * one_if(has_ahead) + 8 * one_if(has_through) + 16 * one_if(has_beyond)

    def step(s, sent):
        word = pick(steps, s >> 1) >> (13 * (s & 1))
        block = word & 127
        slot = block >> 1
        here = (slot <= last_here) | ((slot >= THROUGH * PARTS) & has_beyond)
        ways = jnp.where(here, (word >> 8) & open_ways, 0)

        @pl.when(here & ((word & 128) != 0))
        def _():
            await_copy(parts.at[block], part_sem.at[block])

        @pl.when(ways != 0)
        def _():
            for d in range(DIRS):
                @pl.when((ways & (1 << d)) != 0)
                def _():
                    to = block + 2 * shifts[d]
                    send(parts.at[block], parts.at[to], send_sem.at[d], part_sem.at[to], targets[d])
        for d in range(DIRS):
            sent = sent + (((ways >> d) & 1) << (6 * d))
        return sent

    def unit(u, now, sent, before, scores, scores_before):
        word = pick(units, u)
        slot, end = word & 63, word >> 6
        sent = lax.fori_loop(now, end, step, sent)
        score(slot, slot & (PARTS - 1), scores)
        combine_back(before, scores_before)
        return end, sent, slot

    for p in range(PARTS):
        await_copy(give_kv.at[p], kv_sem.at[p])

    opening = of_place(OPEN)
    sent = lax.fori_loop(0, opening, step, jnp.int32(0))

    loads[2].wait()
    qf[...] = q_in[...].astype(jnp.float32).reshape(tokens * q_heads, HD)

    def queries_of(p, r, side):
        return qf[pl.ds((side * PARTS + p) * group + r, tokens, stride=q_heads), :].T

    for p in range(PARTS):
        for r in range(group):
            give_q[p, :, pl.ds(r * tokens, tokens)] = queries_of(p, r, other).astype(jnp.bfloat16)
        send(give_q.at[p], qx.at[p], q_send, q_sem.at[p], pair)

    scale = LOG2E * HD**-0.5

    def put_queries(p, at_rows, value):
        scaled = value * scale
        high = scaled.astype(jnp.bfloat16)
        qs[p, pl.ds(0, HD), at_rows] = high
        qs[p, pl.ds(HD, HD), at_rows] = (scaled - high.astype(jnp.float32)).astype(jnp.bfloat16)

    for p in range(PARTS):
        for r in range(group):
            put_queries(p, pl.ds(pl.multiple_of(core * rows + r * tokens, tokens), tokens), queries_of(p, r, core))

    def attend_own():
        key = lax.broadcasted_iota(jnp.int32, (BLK, rows), 0)
        query = lax.broadcasted_iota(jnp.int32, (BLK, rows), 1) % tokens
        causal = jnp.where(key <= query, jnp.float32(0), jnp.float32(MASKED))
        biases = [[jnp.float32(0), jnp.float32(MASKED)], [bias_of(1, 1), jnp.float32(0)]]
        for p in range(PARTS):
            await_copy(qx.at[p], q_sem.at[p])
            put_queries(p, pl.ds(pl.multiple_of(other * rows, rows), rows), qx[p].astype(jnp.float32))
        score(0, 0, even)
        for p in range(PARTS):
            if p + 1 < PARTS:
                score(p + 1, p + 1, (even, odd)[(p + 1) % 2])
            combine(p, p, (even, odd)[p % 2], biases, causal)

    attend_own()

    def two_units(i, state):
        state = unit(2 * i, *state, even, odd)
        return unit(2 * i + 1, *state, odd, even)

    _, sent, before = lax.fori_loop(0, len(UNITS) // 2, two_units, (opening, sent, jnp.int32(256)))
    combine_back(before, odd)

    def result(p, r, side):
        at_rows = pl.ds(pl.multiple_of(side * rows + r * tokens, tokens), tokens)
        return (acc[p, pl.ds(0, HD), at_rows] / acc[p, pl.ds(HD, 1), at_rows]).T.astype(jnp.bfloat16)

    for p in range(PARTS):
        for r in range(group):
            give_out[p, :, pl.ds(r * HD, HD)] = result(p, r, other)
        send(give_out.at[p], o_ref.at[:, pl.ds(pl.multiple_of((core * PARTS + p) * rows, rows), rows)], out_send, out_sem, pair)
    for p in range(PARTS):
        for r in range(group):
            place = pl.ds(pl.multiple_of((core * PARTS + p) * rows + r * HD, HD), HD)
            o_ref[:, place] = result(p, r, core)

    for d in range(DIRS):
        for n in range(1, MOST + 1):
            @pl.when(((sent >> (6 * d)) & 63) == n)
            def _():
                await_copy(parts.at[pl.ds(0, n)], send_sem.at[d])
    await_copy(give_kv, kv_send)
    await_copy(give_q, q_send)
    await_copy(give_out, out_send)
    await_copy(give_out, out_sem)


def on_device(queries, keys, values, doc_blocks):
    tokens, q_heads, _ = queries.shape
    kv_heads = keys.shape[1]
    group = q_heads // kv_heads
    rows = group * tokens
    bf16, f32 = jnp.bfloat16, jnp.float32
    anywhere = pl.BlockSpec(memory_space=pl.ANY)
    dma = pltpu.SemaphoreType.DMA
    flat = pl.pallas_call(
        kernel,
        out_shape=jax.ShapeDtypeStruct((tokens, q_heads * HD), bf16),
        in_specs=[anywhere] * 4,
        out_specs=pl.BlockSpec(memory_space=pltpu.VMEM),
        scratch_shapes=[
            pltpu.VMEM(queries.shape, bf16),
            pltpu.VMEM(keys.shape, bf16),
            pltpu.VMEM(values.shape, bf16),
            pltpu.SMEM(doc_blocks.shape, jnp.int32),
            pltpu.VMEM(((THROUGH + 1) * PARTS * 2, 2 * BLK, HD), bf16),
            pltpu.VMEM((PARTS, 2 * BLK, HD), bf16),
            pltpu.VMEM((PARTS, HD, rows), bf16),
            pltpu.VMEM((PARTS, tokens, group * HD), bf16),
            pltpu.VMEM((PARTS, HD, rows), bf16),
            pltpu.VMEM((tokens * q_heads, HD), f32),
            pltpu.VMEM((tokens * kv_heads, HD), f32),
            pltpu.VMEM((tokens * kv_heads, HD), f32),
            pltpu.VMEM((PARTS, 2 * HD, 2 * rows), bf16),
            pltpu.VMEM((PARTS, HD + 16, 2 * rows), f32),
            pltpu.VMEM((PARTS, 8, 2 * rows), f32),
            pltpu.VMEM((2 * BLK, 2 * rows), f32),
            pltpu.VMEM((2 * BLK, 2 * rows), f32),
            dma((4,)),
            dma((DIRS,)),
            dma(((THROUGH + 1) * PARTS * 2,)),
            dma,
            dma((PARTS,)),
            dma,
            dma((PARTS,)),
            dma,
            dma,
        ],
        compiler_params=pltpu.CompilerParams(
            collective_id=0, has_side_effects=True, vmem_limit_bytes=63 << 20
        ),
        name="attend",
    )(queries, keys, values, doc_blocks)
    return flat.reshape(queries.shape)


def solution(mesh):
    placed = P(("ctx", "dp"), None, None)
    return jax.shard_map(
        on_device,
        mesh=mesh,
        in_specs=(placed, placed, placed, P()),
        out_specs=placed,
        check_vma=False,
    )
```

```python
import jax
import jax.numpy as jnp
from jax import lax
from jax.experimental import pallas as pl
from jax.experimental.pallas import tpu as pltpu
from jax.sharding import PartitionSpec as P

STEPS = (
    (2130179, 2105602, 2138372, 2138370, 2097410, 2105606, 8406019, 8422402),
    (4194565, 4210950, 8413441, 8438019, 8413441, 8446210, 16786438, 16802816),
    (4235783, 12608000, 8438786, 8389636, 8446982, 8414210, 16820231, 8446982),
    (8406022, 25224198, 16820225, 16836611, 10520577, 2123781, 8430596, 1164194),
    (16802823, 16787461, 8446211, 2148357, 8429830, 2155520, 35201443, 5460171),
    (16787461, 4202757, 2114560, 10544129, 1147555, 5563396, 5439626, 3441678),
    (4203266, 8430596, 5529739, 5554314, 10588361, 3231949, 8474831, 5439625),
    (35217670, 2155014, 8483017, 8409291, 1155750, 1156101, 35233928, 1131529),
    (2106022, 1339599, 5521664, 1122561, 5563661, 2204322, 5497250, 3695520),
    (3428557, 2384391, 1151181, 35250852, 1581193, 1262593, 1123335, 8430235),
    (9757188, 1360898, 8487174, 35234052, 2171024, 1139363, 3679142, 7651467),
    (9662665, 8679629, 5554317, 5506058, 8708624, 1196229, 8389277, 8413849),
    (4219143, 4505860, 5464769, 5496974, 11625124, 8601867, 5538247, 3465359),
    (1598603, 35201191, 8495367, 2097859, 5546135, 5505166, 1613964, 4513950),
    (1131674, 1344670, 1368202, 1156105, 1294474, 2212875, 4759706, 3523585),
    (4407563, 2417156, 1613982, 1630881, 4440357, 5538448, 3449864, 1302674),
    (8470725, 1630346, 4440330, 2203802, 1115173, 2416783, 1253518, 8536622),
    (2179271, 9666725, 1164315, 1173018, 2122412, 5440530, 8462885, 3481749),
    (9683462, 2392226, 1302688, 1613991, 1221655, 1122469, 1212842, 4440254),
    (1163457, 1147397, 4448551, 2359451, 1163437, 2171429, 1557034, 1205269),
    (3629598, 1615000, 1401895, 1328667, 8560906, 1205264, 3466241, 1278373),
    (8503481, 2195592, 1114249, 1245355, 1172124, 4350113, 1278101, 1230373),
    (1401001, 8454691, 2449952, 4391211, 1548999, 10608780, 8561214, 1286563),
    (13787433, 9625795, 1393672, 1393678, 8618248, 1114270, 3408017, 8544803),
    (1523887, 3498177, 9667244, 1114252, 1400978, 2130106, 1270311, 1434017),
    (1156246, 1557028, 1171723, 4776225, 8536327, 8503866, 3474449, 4448443),
    (5431722, 9552059, 1286829, 1385505, 5808797, 1220753, 4456595, 3556391),
    (3294231, 1540389, 8634658, 4513967, 2212015, 2138795, 8487090, 1540241),
    (9633982, 1253916, 1532051, 9666863, 1328136, 1303582, 1384877, 8471090),
    (3522959, 1172505, 4513942, 1523884, 3564215, 1376434, 4522281, 3580055),
    (9503396, 2179256, 2253829, 2458140, 1483446, 2507807, 8601758, 4702388),
    (5546163, 9585176, 5824658, 1213584, 2220179, 5636774, 1138849, 3712025),
    (1492112, 1376406, 2580644, 4530363, 5735583, 2490547, 2367670, 1441932),
    (1220767, 5398798, 1377289, 1287444, 2482346, 1229836, 8544809, 8659525),
    (1564855, 1188883, 1212611, 1466542, 9660056, 1384623, 1196213, 3563691),
    (1508497, 2236599, 2245156, 12820795, 2138290, 5480751, 4423989, 4423821),
    (3220636, 8519824, 1450172, 1417355, 1598112, 1499310, 8585387, 3728415),
    (9535912, 1425549, 4358335, 2515137, 5513384, 5464356, 7741584, 4628666),
    (3540125, 1564983, 1556774, 1540786, 1261759, 1474750, 8593583, 1393686),
    (1253556, 1139729, 9609394, 2465938, 1212600, 1237285, 3506319, 8626616),
    (1483185, 2220217, 4686130, 1228963, 7823534, 9667263, 8643260, 5710007),
    (1540244, 3219615, 9650341, 9683376, 1524393, 1392908, 1228986, 1410065),
    (1335469, 9601202, 2212541, 5670041, 1228980, 1597612, 4399293, 1418177),
    (1458348, 1467546, 1385623, 5742760, 1441937, 1491200, 1467406, 1212607),
    (1310909, 2474145, 2425007, 1237439, 1556633, 1540283, 4465083, 1114294),
    (161, 3540381, 5677238, 11673749, 1515697, 5742880, 1238036, 1376445),
    (0, 1417365, 2539694, 1491646, 0, 2162869, 8520120, 1450128),
    (0, 1392817, 1475258, 3612819, 0, 1507476, 7807159, 0),
    (0, 1474715, 1499441, 1499301, 0, 1630381, 1155263, 0),
    (0, 1433772, 1187984, 1507505, 0, 1253553, 1597614, 0),
    (0, 1482938, 1253528, 181, 0, 1581241, 1441972, 0),
    (0, 1548448, 1507504, 0, 0, 0, 0, 0),
    (0, 1384630, 1515699, 0, 0, 0, 0, 0),
    (0, 0, 161, 0, 0, 0, 0, 0),
)
UNITS = (
    (1427, 1747, 1169, 1761, 1030, 1361, 1105, 1185),
    (1825, 2211, 1478, 2000, 1171, 1477, 1284, 1293),
    (1869, 2322, 1696, 2147, 1312, 1698, 1440, 1413),
    (2053, 2577, 1861, 2311, 1810, 2119, 1635, 1548),
    (2210, 2722, 2003, 2515, 1861, 2386, 1826, 1671),
    (2403, 3041, 2274, 2658, 2180, 2697, 2066, 1875),
    (2528, 3168, 2447, 2765, 2518, 2896, 2188, 2063),
    (3229, 3724, 2820, 3093, 2823, 2950, 2707, 2569),
    (3413, 3847, 3093, 3142, 2915, 3140, 2762, 2642),
    (3467, 4171, 3335, 3396, 3406, 3400, 2958, 2897),
    (3593, 4361, 3478, 4189, 3554, 3727, 3213, 2958),
    (3783, 4680, 3598, 4366, 3729, 4051, 3732, 3152),
    (3863, 4806, 4041, 4503, 3931, 4185, 3919, 3223),
    (4114, 5023, 4195, 4677, 4041, 4500, 4048, 3787),
    (4303, 5125, 4449, 4822, 4175, 4695, 4101, 3930),
    (4443, 5276, 5023, 4896, 4318, 4877, 4489, 4130),
    (4511, 5327, 5130, 5081, 4373, 5131, 4693, 4505),
    (4552, 5444, 5330, 5201, 4569, 5279, 4808, 4550),
    (4636, 5657, 5453, 5391, 4769, 5326, 5063, 4771),
    (4740, 5838, 5534, 5516, 4880, 5525, 5142, 4829),
    (4820, 5962, 5707, 5588, 5005, 5601, 5470, 5013),
    (4870, 6104, 5780, 5726, 5130, 5723, 5657, 5276),
    (5006, 6165, 5975, 5771, 5271, 5853, 5725, 5472),
    (5132, 6221, 6109, 5898, 5332, 5982, 5899, 5526),
    (5208, 6358, 6170, 6024, 5405, 6042, 6107, 5599),
    (5274, 6423, 6299, 6175, 5466, 6154, 6172, 5642),
    (5386, 6493, 6408, 6217, 5515, 6230, 6239, 5723),
    (5585, 6554, 6540, 6290, 5576, 6307, 6278, 5764),
    (5718, 6672, 6616, 6427, 5708, 6360, 6359, 5918),
    (5785, 6750, 6745, 6424, 5791, 6412, 6433, 5972),
    (5854, 6747, 6812, 6428, 5848, 6492, 6490, 6024),
    (5840, 6804, 6864, 6490, 5916, 6560, 6552, 6040),
)
OPEN = (15, 16, 12, 12, 10, 11, 8, 6)
MOST = 23
PARTS = 4
BACK = 8
THROUGH = 9
DIRS = 5
BLK = 128
HD = 128
LOG2E = 1.4426950408889634
MASKED = -1e30
MESH = pl.DeviceIdType.MESH


def kernel(
    q_hbm, k_hbm, v_hbm, docs_hbm, o_ref,
    q_in, k_in, v_in, docs, parts, give_kv, give_q, give_out, qx, qf, kf, vf, qs, acc, top, even, odd,
    load_sem, send_sem, part_sem, kv_send, kv_sem, q_send, q_sem, out_send, out_sem,
):
    tokens, q_heads, _ = q_in.shape
    kv_heads = k_in.shape[1]
    group = q_heads // kv_heads
    rows = group * tokens
    dp = lax.axis_index("dp")
    z = lax.axis_index("ctx")
    planes = lax.axis_size("ctx")
    x, y, core = dp // 8, (dp // 2) % 4, dp % 2
    chip = dp // 2
    other = 1 - core

    def one_if(condition):
        return jnp.where(condition, jnp.int32(1), jnp.int32(0))

    def at(to_x, to_y, to_z, to_core):
        return ((to_x % 4) * 8 + (to_y % 4) * 2 + to_core, to_z)

    loads = [
        pltpu.make_async_copy(src, dst, load_sem.at[i])
        for i, (src, dst) in enumerate(((k_hbm, k_in), (v_hbm, v_in), (q_hbm, q_in), (docs_hbm, docs)))
    ]
    for load in loads:
        load.start()

    over_ahead = one_if(x == 3)
    over_beyond = one_if((x == 1) | (x == 2))
    has_ahead = z + over_ahead < planes
    has_behind = z - one_if(x == 0) >= 0
    has_beyond = z + over_beyond < planes
    has_beyond_from = z - one_if(x <= 1) >= 0
    has_through = z + one_if(x >= 2) < planes
    pair = at(x, y, z, other)
    up = at(x, y + 1, z, core)
    down = at(x, y + 3, z, core)
    ahead = at(x + 1, y, z + over_ahead, core)
    through = at(x + 3, y, z, core)

    last_here = PARTS * jnp.where(z > 0, jnp.int32(BACK), jnp.minimum(chip, BACK)) + PARTS - 1

    def clear(slot, c):
        parts[slot] = jnp.zeros((2 * BLK, HD), jnp.bfloat16)
        return c
    lax.fori_loop(2 * (last_here + 1), 2 * (BACK + 1) * PARTS, clear, 0)
    for p in range(PARTS):
        clear(2 * (BACK * PARTS + p), 0)

    barrier = pltpu.get_barrier_semaphore()

    def greet(device):
        pl.semaphore_signal(barrier, inc=1, device_id=device, device_id_type=MESH)

    for friend in (pair, up, down, through, at(x + 1, y, z, core)):
        greet(friend)
    maybe = (
        (has_ahead, ahead),
        (has_behind, at(x + 3, y, z - one_if(x == 0), core)),
        (has_beyond, at(x + 3, y, z + over_beyond, core)),
        (has_beyond_from, at(x + 1, y, z - one_if(x <= 1), core)),
    )
    greeted = jnp.int32(5)
    for there, friend in maybe:
        greeted = greeted + one_if(there)
        pl.when(there)(lambda friend=friend: greet(friend))

    def of_place(entry):
        pairs = [jnp.where(core == 0, jnp.int32(entry[2 * i]), jnp.int32(entry[2 * i + 1])) for i in range(4)]
        return jnp.where(y < 2, jnp.where(y == 0, pairs[0], pairs[1]), jnp.where(y == 2, pairs[2], pairs[3]))

    steps = [of_place(entry) for entry in STEPS]
    units = [of_place(entry) for entry in UNITS]

    def pick(values, index):
        while len(values) > 1:
            low = (index & 1) == 0
            values = [
                jnp.where(low, values[i], values[i + 1]) if i + 1 < len(values) else values[i]
                for i in range(0, len(values), 2)
            ]
            index = index >> 1
        return values[0]

    loads[0].wait()
    kf[...] = k_in[...].astype(jnp.float32).reshape(tokens * kv_heads, HD)
    loads[1].wait()
    vf[...] = v_in[...].astype(jnp.float32).reshape(tokens * kv_heads, HD)
    for p in range(PARTS):
        head = pl.ds(other * PARTS + p, tokens, stride=kv_heads)
        give_kv[p, pl.ds(0, BLK), :] = kf[head, :].astype(jnp.bfloat16)
        give_kv[p, pl.ds(BLK, BLK), :] = vf[head, :].T.astype(jnp.bfloat16)
    for p in range(PARTS):
        head = pl.ds(core * PARTS + p, tokens, stride=kv_heads)
        parts[2 * p + core, pl.ds(0, BLK), :] = kf[head, :].astype(jnp.bfloat16)
        parts[2 * p + core, pl.ds(BLK, BLK), :] = vf[head, :].T.astype(jnp.bfloat16)

    pl.semaphore_wait(barrier, greeted)

    def send(src, dst, sem, landed, device):
        pltpu.make_async_remote_copy(
            src_ref=src, dst_ref=dst, send_sem=sem, recv_sem=landed, device_id=device, device_id_type=MESH
        ).start()

    def await_copy(ref, sem):
        pltpu.make_async_copy(ref, ref, sem).wait()

    for p in range(PARTS):
        send(give_kv.at[p], parts.at[2 * p + core], kv_send, kv_sem.at[p], pair)

    loads[3].wait()
    reach = []
    for b in range(2):
        block = (z * 16 + chip) * 2 + b
        end = jnp.int32(0)
        start = jnp.int32(0)
        for i in range(docs.shape[0]):
            end = end + docs[i]
            start = jnp.where(end <= block, end, start)
        reach.append(block - start)

    def bias_of(back, b):
        return jnp.where(back <= reach[b], jnp.float32(0), jnp.float32(MASKED))

    ones = jnp.ones((16, 2 * BLK), jnp.bfloat16)

    def score(slot, p, into):
        keys = jnp.concatenate([parts[2 * slot, pl.ds(0, BLK), :], parts[2 * slot + 1, pl.ds(0, BLK), :]], axis=0)
        keys = jnp.concatenate([keys, keys], axis=1)
        for b in range(2):
            at_rows = pl.ds(b * rows, rows)
            into[:, at_rows] = jnp.dot(keys, qs[p, :, at_rows], preferred_element_type=jnp.float32)

    def combine(slot, p, scores, biases, causal=None):
        values = jnp.concatenate([parts[2 * slot, pl.ds(BLK, BLK), :], parts[2 * slot + 1, pl.ds(BLK, BLK), :]], axis=1)
        values = jnp.concatenate([values, ones], axis=0)
        for b in range(2):
            at_rows = pl.ds(b * rows, rows)
            halves = [scores[pl.ds(h * BLK, BLK), at_rows] for h in range(2)]
            if causal is not None:
                halves[b] = halves[b] + causal
            peaks = [jnp.max(halves[h], axis=0, keepdims=True) + biases[b][h] for h in range(2)]
            new_top = jnp.maximum(peaks[0], peaks[1])
            if causal is None:
                old_top = top[p, pl.ds(0, 1), at_rows]
                new_top = jnp.maximum(old_top, new_top)
            weights = [jnp.exp2(halves[h] - (new_top - biases[b][h])).astype(jnp.bfloat16) for h in range(2)]
            summed = jnp.dot(values, jnp.concatenate(weights, axis=0), preferred_element_type=jnp.float32)
            if causal is None:
                acc[p, :, at_rows] = acc[p, :, at_rows] * jnp.exp2(old_top - new_top) + summed
            else:
                acc[p, :, at_rows] = summed
            top[p, pl.ds(0, 1), at_rows] = new_top

    def combine_back(code, scores):
        k, p = code >> 2, code & (PARTS - 1)
        biases = [[bias_of(2 * k + b - h, b) for h in range(2)] for b in range(2)]
        combine(code & 63, p, scores, biases)

    shifts = (
        PARTS * jnp.where(y == 3, jnp.int32(-3), jnp.int32(1)),
        PARTS * jnp.where(y == 0, jnp.int32(3), jnp.int32(-1)),
        4 * PARTS,
        THROUGH * PARTS,
        (BACK - THROUGH) * PARTS,
    )
    targets = (up, down, ahead, through, at(x + 3, y, z + over_beyond, core))
    open_ways = 3 + 4 * one_if(has_ahead) + 8 * one_if(has_through) + 16 * one_if(has_beyond)

    def step(s, sent):
        word = pick(steps, s >> 1) >> (13 * (s & 1))
        block = word & 127
        slot = block >> 1
        here = (slot <= last_here) | ((slot >= THROUGH * PARTS) & has_beyond)
        ways = jnp.where(here, (word >> 8) & open_ways, 0)

        @pl.when(here & ((word & 128) != 0))
        def _():
            await_copy(parts.at[block], part_sem.at[block])

        @pl.when(ways != 0)
        def _():
            for d in range(DIRS):
                @pl.when((ways & (1 << d)) != 0)
                def _():
                    to = block + 2 * shifts[d]
                    send(parts.at[block], parts.at[to], send_sem.at[d], part_sem.at[to], targets[d])
        for d in range(DIRS):
            sent = sent + (((ways >> d) & 1) << (6 * d))
        return sent

    def unit(u, now, sent, before, scores, scores_before):
        word = pick(units, u)
        slot, end = word & 63, word >> 6
        sent = lax.fori_loop(now, end, step, sent)
        score(slot, slot & (PARTS - 1), scores)
        combine_back(before, scores_before)
        return end, sent, slot

    for p in range(PARTS):
        await_copy(give_kv.at[p], kv_sem.at[p])

    opening = of_place(OPEN)
    sent = lax.fori_loop(0, opening, step, jnp.int32(0))

    loads[2].wait()
    qf[...] = q_in[...].astype(jnp.float32).reshape(tokens * q_heads, HD)

    def queries_of(p, r, side):
        return qf[pl.ds((side * PARTS + p) * group + r, tokens, stride=q_heads), :].T

    for p in range(PARTS):
        for r in range(group):
            give_q[p, :, pl.ds(r * tokens, tokens)] = queries_of(p, r, other).astype(jnp.bfloat16)
        send(give_q.at[p], qx.at[p], q_send, q_sem.at[p], pair)

    scale = LOG2E * HD**-0.5

    def put_queries(p, at_rows, value):
        scaled = value * scale
        high = scaled.astype(jnp.bfloat16)
        qs[p, pl.ds(0, HD), at_rows] = high
        qs[p, pl.ds(HD, HD), at_rows] = (scaled - high.astype(jnp.float32)).astype(jnp.bfloat16)

    for p in range(PARTS):
        for r in range(group):
            put_queries(p, pl.ds(pl.multiple_of(core * rows + r * tokens, tokens), tokens), queries_of(p, r, core))

    def attend_own():
        key = lax.broadcasted_iota(jnp.int32, (BLK, rows), 0)
        query = lax.broadcasted_iota(jnp.int32, (BLK, rows), 1) % tokens
        causal = jnp.where(key <= query, jnp.float32(0), jnp.float32(MASKED))
        biases = [[jnp.float32(0), jnp.float32(MASKED)], [bias_of(1, 1), jnp.float32(0)]]
        for p in range(PARTS):
            await_copy(qx.at[p], q_sem.at[p])
            put_queries(p, pl.ds(pl.multiple_of(other * rows, rows), rows), qx[p].astype(jnp.float32))
        score(0, 0, even)
        for p in range(PARTS):
            if p + 1 < PARTS:
                score(p + 1, p + 1, (even, odd)[(p + 1) % 2])
            combine(p, p, (even, odd)[p % 2], biases, causal)

    attend_own()

    def two_units(i, state):
        state = unit(2 * i, *state, even, odd)
        return unit(2 * i + 1, *state, odd, even)

    _, sent, before = lax.fori_loop(0, len(UNITS) // 2, two_units, (opening, sent, jnp.int32(256)))
    combine_back(before, odd)

    def result(p, r, side):
        at_rows = pl.ds(pl.multiple_of(side * rows + r * tokens, tokens), tokens)
        return (acc[p, pl.ds(0, HD), at_rows] / acc[p, pl.ds(HD, 1), at_rows]).T.astype(jnp.bfloat16)

    for p in range(PARTS):
        for r in range(group):
            give_out[p, :, pl.ds(r * HD, HD)] = result(p, r, other)
        send(give_out.at[p], o_ref.at[:, pl.ds(pl.multiple_of((core * PARTS + p) * rows, rows), rows)], out_send, out_sem, pair)
    for p in range(PARTS):
        for r in range(group):
            place = pl.ds(pl.multiple_of((core * PARTS + p) * rows + r * HD, HD), HD)
            o_ref[:, place] = result(p, r, core)

    for d in range(DIRS):
        for n in range(1, MOST + 1):
            @pl.when(((sent >> (6 * d)) & 63) == n)
            def _():
                await_copy(parts.at[pl.ds(0, n)], send_sem.at[d])
    await_copy(give_kv, kv_send)
    await_copy(give_q, q_send)
    await_copy(give_out, out_send)
    await_copy(give_out, out_sem)


def on_device(queries, keys, values, doc_blocks):
    tokens, q_heads, _ = queries.shape
    kv_heads = keys.shape[1]
    group = q_heads // kv_heads
    rows = group * tokens
    bf16, f32 = jnp.bfloat16, jnp.float32
    anywhere = pl.BlockSpec(memory_space=pl.ANY)
    dma = pltpu.SemaphoreType.DMA
    flat = pl.pallas_call(
        kernel,
        out_shape=jax.ShapeDtypeStruct((tokens, q_heads * HD), bf16),
        in_specs=[anywhere] * 4,
        out_specs=pl.BlockSpec(memory_space=pltpu.VMEM),
        scratch_shapes=[
            pltpu.VMEM(queries.shape, bf16),
            pltpu.VMEM(keys.shape, bf16),
            pltpu.VMEM(values.shape, bf16),
            pltpu.SMEM(doc_blocks.shape, jnp.int32),
            pltpu.VMEM(((THROUGH + 1) * PARTS * 2, 2 * BLK, HD), bf16),
            pltpu.VMEM((PARTS, 2 * BLK, HD), bf16),
            pltpu.VMEM((PARTS, HD, rows), bf16),
            pltpu.VMEM((PARTS, tokens, group * HD), bf16),
            pltpu.VMEM((PARTS, HD, rows), bf16),
            pltpu.VMEM((tokens * q_heads, HD), f32),
            pltpu.VMEM((tokens * kv_heads, HD), f32),
            pltpu.VMEM((tokens * kv_heads, HD), f32),
            pltpu.VMEM((PARTS, 2 * HD, 2 * rows), bf16),
            pltpu.VMEM((PARTS, HD + 16, 2 * rows), f32),
            pltpu.VMEM((PARTS, 8, 2 * rows), f32),
            pltpu.VMEM((2 * BLK, 2 * rows), f32),
            pltpu.VMEM((2 * BLK, 2 * rows), f32),
            dma((4,)),
            dma((DIRS,)),
            dma(((THROUGH + 1) * PARTS * 2,)),
            dma,
            dma((PARTS,)),
            dma,
            dma((PARTS,)),
            dma,
            dma,
        ],
        compiler_params=pltpu.CompilerParams(
            collective_id=0, has_side_effects=True, vmem_limit_bytes=63 << 20
        ),
        name="attend",
    )(queries, keys, values, doc_blocks)
    return flat.reshape(queries.shape)


def solution(mesh):
    placed = P(("ctx", "dp"), None, None)
    return jax.shard_map(
        on_device,
        mesh=mesh,
        in_specs=(placed, placed, placed, P()),
        out_specs=placed,
        check_vma=False,
    )
```
